256 devices in a mesh: chan: 32 (over y, x, core), band: 8 (over z).
Axes of the slice: x: 4, y: 4, z: 8, core: 2. Of those that a mesh axis runs over, the one named last changes fastest.
Arguments:
- spectra: bfloat16 [2, 30, 512, 8192], P(None, None, 'chan', 'band'), may hold values from -6 to 6
- source_block: int32 [1], replicated, may hold values from 0 to 127
- segment_flags: int32 [30], replicated, may hold values from 0 to 1, as said below
Outputs:
- correlations: float32 [64, 8, 1024, 1024], P(None, 'band', 'chan')
The draws below stay inside these ranges and needn't reach their ends.
Inputs may be any that keep to these rules, and one draw needn't show every extreme that they name: `segment_flags`: at least one segment is valid.
All inputs are finite; a program needn't handle non-finite values.
Results may differ from the reference program's by a relative error of at most 0.0037.
Values may be sent and summed in bfloat16 or wider, within the bound.
A program may use at most 128 MiB of HBM per device.

```python
import math
import jax
import jax.numpy as jnp
from jax import lax

LAGS = 1024
F = 512
SEG = 30
SRC = 64
RB = 1024
GROUPS = 8
CH = 8192


def draw_segment_flags(key, part):
    first_key, second_key = jax.random.split(jax.random.fold_in(key, 17))
    random_bits = jax.random.randint(first_key, (SEG,), 0, 2)
    chosen = jax.random.randint(second_key, (), 0, SEG)
    forced = (jnp.arange(SEG) == chosen).astype(jnp.int32)
    return jnp.maximum(random_bits, forced).astype(jnp.int32)


def block_levels(stream_key, extent, cuts, least, high):
    level = 1.0
    for dim, shards_of in cuts:
        heights = jax.random.uniform(jax.random.fold_in(jax.random.fold_in(stream_key, 6), dim), (shards_of,), jnp.float32, least / len(cuts), high / len(cuts))
        level = level * jnp.repeat(jnp.exp(heights), extent[dim] // shards_of).reshape((-1,) + (1,) * (len(extent) - 1 - dim))
    return level


def bell_draw(rng, extent, width, most, cuts=(), kind=jnp.bfloat16):
    values = jax.random.normal(rng, extent, jnp.float32) * width
    if len(cuts) > 0:
        values = block_levels(rng, extent, cuts, -0.22, 0.18) * values
    return jnp.clip(values, min=-most, max=most).astype(kind)


def setup_inputs(seed: int = 0) -> dict:
    key_list = jax.random.split(jax.random.key(seed), 4)
    return {
        "spectra": bell_draw(key_list[0], (2, SEG, F, CH), 1.0, 6.0, ((2, 32), (3, 8))),
        "source_block": jax.random.randint(key_list[1], (1,), 0, CH // SRC).astype(jnp.int32),
        "segment_flags": draw_segment_flags(jax.random.fold_in(key_list[3], 71), 0),
    }


def lag_table():
    frequency = jnp.arange(F, dtype=jnp.int32)[:, None]
    shifted_lag = jnp.arange(LAGS, dtype=jnp.int32)[None, :] - LAGS // 2
    phase_index = frequency * shifted_lag % LAGS
    phase_angle = 2.0 * math.pi / LAGS * phase_index.astype(jnp.float32)
    weight = jnp.where(frequency == 0, 1.0, 2.0).astype(jnp.float32) / jnp.sqrt(jnp.float32(2 * F))
    cosine_component = weight * jnp.cos(phase_angle)
    sin_part = -weight * jnp.sin(phase_angle)
    return jnp.stack([cosine_component, sin_part], axis=1).astype(jnp.bfloat16)

def reference(spectra, source_block, segment_flags):
    first_channel = (source_block[0] * SRC).astype(jnp.int32)
    source = lax.dynamic_slice_in_dim(spectra, first_channel, SRC, 3).astype(jnp.float32)
    valid_mask = segment_flags.astype(jnp.float32)
    valid_window_count = jnp.sum(valid_mask)
    masked = source * valid_mask[None, :, None, None]
    left_real = jnp.concatenate([masked[0], masked[1]], axis=0)
    left_imaginary = jnp.concatenate([masked[1], -masked[0]], axis=0)
    left_operand = jnp.concatenate([left_real, left_imaginary], axis=2)
    lag_weights = lag_table().astype(jnp.float32)

    def one_group(group_index):
        start = (group_index * RB).astype(jnp.int32)
        receiver_traces = lax.dynamic_slice_in_dim(spectra, start, RB, 3)
        receiver_traces = receiver_traces.reshape(2 * SEG, F, RB).astype(jnp.float32)
        cross_spectrum_product = jnp.einsum('kcb,kcp->cbp', left_operand, receiver_traces) / valid_window_count
        cross_spectrum_product = cross_spectrum_product.astype(jnp.bfloat16).reshape(F, 2, SRC, RB).astype(jnp.float32)
        return jnp.einsum('fcsr,fcl->srl', cross_spectrum_product, lag_weights)
    stacked = lax.map(one_group, jnp.arange(GROUPS, dtype=jnp.int32))
    return jnp.transpose(stacked, (1, 0, 2, 3))
```

```python
import functools
import math

import jax
import jax.numpy as jnp
from jax import lax
from jax.experimental import pallas as pl
from jax.experimental.pallas import tpu as pltpu
from jax.sharding import PartitionSpec as P

LAGS = 1024
SEG = 30
SRC = 64
BINS = 16
RX = 32
MESH = pl.DeviceIdType.MESH


def lag_table(bands, chans):
    per = BINS // bands
    bins = BINS * chans
    row = jnp.arange(bins, dtype=jnp.int32)
    frequency = row % chans * BINS + row // (per * chans) * per + row // chans % per
    frequency = frequency[:, None]
    lag = jnp.arange(LAGS, dtype=jnp.int32)[None, :] - LAGS // 2
    phase = 2.0 * math.pi / LAGS * (frequency * lag % LAGS).astype(jnp.float32)
    weight = jnp.where(frequency == 0, 1.0, 2.0).astype(jnp.float32) / jnp.sqrt(jnp.float32(LAGS))
    return jnp.concatenate([weight * jnp.cos(phase), -weight * jnp.sin(phase)], axis=0).astype(jnp.bfloat16)


def pack_kernel(tiles, chans, bands, band_ref, block_ref, flags_ref, x_ref, xs_ref, cand_ref, scale_ref, following):
    segs = 8 * tiles
    depth = BINS * segs
    rows = BINS // bands * segs
    f32, bf16 = jnp.float32, jnp.bfloat16

    following[SEG] = SEG

    def link(i, valid):
        g = SEG - 1 - i
        following[g] = jnp.where(flags_ref[g] > 0, g, following[g + 1])
        return valid + flags_ref[g]

    valid = lax.fori_loop(0, SEG, link, 0)

    def pack(k, at):
        g = jnp.minimum(at, SEG - 1)
        place = pl.ds(pl.multiple_of(k * BINS, BINS), BINS)
        xs_ref[0, place, :] = x_ref[0, g]
        xs_ref[1, place, :] = x_ref[1, g]
        return following[jnp.minimum(at + 1, SEG)]

    lax.fori_loop(0, segs, pack, following[0])

    r_i = lax.broadcasted_iota(jnp.int32, (depth, depth), 0)
    c_i = lax.broadcasted_iota(jnp.int32, (depth, depth), 1)
    to_bins = (r_i == (c_i & (BINS - 1)) * segs + (c_i >> 4)).astype(bf16)

    first = block_ref[0] * SRC
    width = RX * chans
    owner = first // width
    within = first - owner * width
    lane0 = pl.multiple_of(within // 128 * 128, 128)
    upper = (within // SRC) % 2
    sr = xs_ref[0, :, pl.ds(lane0, 128)].astype(f32)
    si = xs_ref[1, :, pl.ds(lane0, 128)].astype(f32)
    lane = lax.broadcasted_iota(jnp.int32, (depth, 128), 1)
    slot = lax.broadcasted_iota(jnp.int32, (depth, 128), 0) >> 4
    low = jnp.where(lane < SRC, sr, pltpu.roll(si, SRC, 1))
    high = jnp.where(lane < SRC, pltpu.roll(sr, SRC, 1), si)
    mine = jnp.where(upper == 0, low, high)
    count = jnp.where(owner == band_ref[0], valid, 0)
    mine = jnp.where(slot < count, mine, 0.0).astype(bf16)
    cand_ref[...] = jnp.dot(to_bins, mine, preferred_element_type=f32).astype(bf16).reshape(bands, rows, 128)
    scale_ref[...] = 1.0 / jnp.full((8, 128), valid, jnp.int32).astype(f32)


def stack_kernel(
    tiles, chans, bands,
    xs, cand, scale_ref, out_ref,
    send, recv, parts, zall, wide, cross,
    a2a_send, a2a_recv, rs_send, rs_recv, ag_send, ag_recv,
    right_send, right_recv, left_send, left_recv, sib_send, sib_recv,
):
    segs = 8 * tiles
    depth = BINS * segs
    per = BINS // bands
    rows = per * segs
    half = chans // 2
    c = lax.axis_index("chan")
    b = lax.axis_index("band")
    f32, bf16 = jnp.float32, jnp.bfloat16

    barrier = pltpu.get_barrier_semaphore()

    def greet_chan(i, carry):
        pl.semaphore_signal(barrier, inc=1, device_id=(lax.rem(c + i, chans), b), device_id_type=MESH)
        return carry

    def greet_band(i, carry):
        pl.semaphore_signal(barrier, inc=1, device_id=(c, lax.rem(b + i, bands)), device_id_type=MESH)
        return carry

    lax.fori_loop(1, chans, greet_chan, 0)
    lax.fori_loop(1, bands, greet_band, 0)

    c_i = lax.broadcasted_iota(jnp.int32, (depth, depth), 1)
    r_i = lax.broadcasted_iota(jnp.int32, (depth, depth), 0)
    from_segs = (c_i == (r_i & (BINS - 1)) * segs + (r_i >> 4)).astype(bf16)

    pl.semaphore_wait(barrier, chans + bands - 2)

    def rs_copy(other, slot_):
        return pltpu.make_async_remote_copy(
            src_ref=cand.at[other], dst_ref=parts.at[slot_],
            send_sem=rs_send.at[other], recv_sem=rs_recv.at[slot_],
            device_id=(c, other), device_id_type=MESH)

    def rs_start(i, carry):
        rs_copy(lax.rem(b + i, bands), b).start()
        return carry

    lax.fori_loop(1, bands, rs_start, 0)

    def a2a_copy(dest, origin):
        return pltpu.make_async_remote_copy(
            src_ref=send.at[dest], dst_ref=recv.at[origin],
            send_sem=a2a_send.at[dest], recv_sem=a2a_recv.at[origin],
            device_id=(dest, b), device_id_type=MESH)

    groups = chans // 4

    def turn(i, carry):
        block = lax.rem(c // 4 + i, groups)
        lanes = pl.ds(pl.multiple_of(block * 128, 128), 128)
        for comp in range(2):
            turned = jnp.dot(xs[comp, :, lanes].T, from_segs, preferred_element_type=f32).astype(bf16)
            for q in range(4):
                send[4 * block + q, comp * RX:(comp + 1) * RX, :] = turned[q * RX:(q + 1) * RX]
        for q in range(4):
            dest = 4 * block + q

            @pl.when(dest != c)
            def _():
                a2a_copy(dest, c).start()
        return carry

    lax.fori_loop(0, groups, turn, 0)
    recv[c] = send[c]

    def rs_sum(i, total):
        other = lax.rem(b + i, bands)
        rs_copy(other, other).wait_recv()
        return total + parts[other].astype(f32)

    zall[b, c] = lax.fori_loop(1, bands, rs_sum, cand[b].astype(f32)).astype(bf16)

    def ag_copy(dest, origin):
        return pltpu.make_async_remote_copy(
            src_ref=zall.at[b, origin], dst_ref=zall.at[b, origin],
            send_sem=ag_send.at[dest], recv_sem=ag_recv.at[origin],
            device_id=(dest, b), device_id_type=MESH)

    def ag_start(i, carry):
        ag_copy(lax.rem(c + i, chans), c).start()
        return carry

    lax.fori_loop(1, chans, ag_start, 0)

    def ag_wait(i, carry):
        other = lax.rem(c + i, chans)
        ag_copy(other, other).wait_recv()
        return carry

    lax.fori_loop(1, chans, ag_wait, 0)

    core = lax.rem(c, 2)
    twin = c + 1 - 2 * core
    right = lax.rem(b + 1, bands)
    left = lax.rem(b + bands - 1, bands)
    last = bands // 2

    def piece(origin, start, size):
        return zall.at[origin, pl.ds(start, size)]

    def hop(step, way, which):
        origin = lax.rem(b + bands - way * (step - 1 + which), bands)
        start, size = half * core, half
        if step == last:
            size = half // 2
            if way < 0:
                start = start + size
        ref = piece(origin, start, size)
        sems = (right_send, right_recv) if way > 0 else (left_send, left_recv)
        return pltpu.make_async_remote_copy(
            src_ref=ref, dst_ref=ref, send_sem=sems[0].at[step - 1], recv_sem=sems[1].at[step - 1],
            device_id=(c, right if way > 0 else left), device_id_type=MESH)

    def share(step, way, own):
        origin = lax.rem(b + bands - way * step, bands)
        start, size = half * (core if own else 1 - core), half
        if step == last:
            size = half // 2
            if way < 0:
                start = start + size
        ref = piece(origin, start, size)
        k = 2 * (step - 1) + (0 if way > 0 else 1)
        return pltpu.make_async_remote_copy(
            src_ref=ref, dst_ref=ref, send_sem=sib_send.at[k], recv_sem=sib_recv.at[k],
            device_id=(twin, b), device_id_type=MESH)

    wide[...] = jnp.zeros_like(wide)
    inverse = jnp.broadcast_to(scale_ref[0:1, :], (RX, 128))
    sign = jnp.where(lax.broadcasted_iota(jnp.int32, (RX, 128), 1) < SRC, inverse, -inverse)
    row_bin = lax.broadcasted_iota(jnp.int32, (rows, 128), 0)

    def stack(origin):
        place = pl.ds(pl.multiple_of(origin * rows, rows), rows)

        def chunk(j, carry):
            z = zall[origin, j]
            for p in range(per):
                inside = (row_bin >= p * segs) & (row_bin < (p + 1) * segs)
                wide[place, p * 128:(p + 1) * 128] = jnp.where(inside, z, jnp.zeros_like(z))
            product = jnp.dot(recv[j], wide[...], preferred_element_type=f32)
            for p in range(per):
                same = product[:RX, p * 128:(p + 1) * 128]
                swapped = pltpu.roll(product[RX:, p * 128:(p + 1) * 128], SRC, 1)
                cross[origin * (per * chans) + p * chans + j] = same * inverse + swapped * sign
            return carry

        lax.fori_loop(0, chans, chunk, 0)
        wide[place, :] = jnp.zeros((rows, per * 128), bf16)

    def a2a_wait(i, carry):
        other = lax.rem(c + i, chans)
        a2a_copy(other, other).wait_recv()
        return carry

    for step in range(1, last + 1):
        for way in (1, -1):
            hop(step, way, 0).start()
        for way in (1, -1):
            hop(step, way, 1).wait_recv()
            share(step, way, True).start()

    lax.fori_loop(1, chans, a2a_wait, 0)
    for step in range(1, last + 1):
        for way in (1, -1):
            share(step, way, False).wait_recv()

    def stack_all(i, carry):
        stack(i)
        return carry

    lax.fori_loop(0, bands, stack_all, 0)

    bins = BINS * chans

    def turn_back(r, carry):
        flat = cross[:, r, :].astype(bf16).T
        out_ref[r // 8, lax.rem(r, 8), :, :bins] = flat[:SRC]
        out_ref[r // 8, lax.rem(r, 8), :, bins:] = flat[SRC:]
        return carry

    lax.fori_loop(0, RX, turn_back, 0)

    def rs_done(i, carry):
        rs_copy(lax.rem(b + i, bands), b).wait_send()
        return carry

    def chan_done(i, carry):
        other = lax.rem(c + i, chans)
        a2a_copy(other, c).wait_send()
        ag_copy(other, c).wait_send()
        return carry

    lax.fori_loop(1, bands, rs_done, 0)
    lax.fori_loop(1, chans, chan_done, 0)
    for step in range(1, last + 1):
        for way in (1, -1):
            hop(step, way, 0).wait_send()
            share(step, way, True).wait_send()


def stacked(tiles, chans, bands, block, flags, x):
    segs = 8 * tiles
    depth = BINS * segs
    per = BINS // bands
    rows = per * segs
    bins = BINS * chans
    last = bands // 2
    dma = pltpu.SemaphoreType.DMA
    bf16 = jnp.bfloat16
    flops = 2 * chans * bands * 2 * RX * depth * per * 128
    vmem = pl.BlockSpec(memory_space=pltpu.VMEM)
    smem = pl.BlockSpec(memory_space=pltpu.SMEM)
    packed = pl.pallas_call(
        functools.partial(pack_kernel, tiles, chans, bands),
        out_shape=(
            jax.ShapeDtypeStruct((2, depth, RX * chans), bf16),
            jax.ShapeDtypeStruct((bands, rows, 128), bf16),
            jax.ShapeDtypeStruct((8, 128), jnp.float32),
        ),
        in_specs=[smem, smem, smem, vmem],
        out_specs=(vmem, vmem, vmem),
        scratch_shapes=[pltpu.SMEM((32,), jnp.int32)],
        compiler_params=pltpu.CompilerParams(vmem_limit_bytes=24 * 1024 * 1024),
    )(lax.axis_index("band").reshape(1), block, flags, x)
    return pl.pallas_call(
        functools.partial(stack_kernel, tiles, chans, bands),
        out_shape=jax.ShapeDtypeStruct((RX // 8, 8, SRC, 2 * bins), bf16),
        in_specs=[vmem] * 3,
        out_specs=vmem,
        scratch_shapes=[
            pltpu.VMEM((chans, 2 * RX, depth), bf16),
            pltpu.VMEM((chans, 2 * RX, depth), bf16),
            pltpu.VMEM((bands, rows, 128), bf16),
            pltpu.VMEM((bands, chans, rows, 128), bf16),
            pltpu.VMEM((depth, per * 128), bf16),
            pltpu.VMEM((bins, RX, 128), jnp.float32),
            dma((chans,)), dma((chans,)), dma((bands,)), dma((bands,)), dma((chans,)), dma((chans,)),
            dma((last,)), dma((last,)), dma((last,)), dma((last,)), dma((2 * last,)), dma((2 * last,)),
        ],
        compiler_params=pltpu.CompilerParams(
            collective_id=tiles, has_side_effects=True, vmem_limit_bytes=48 * 1024 * 1024
        ),
        cost_estimate=pl.CostEstimate(flops=flops, bytes_accessed=8 * 1024 * 1024, transcendentals=0),
    )(*packed)


def lag_kernel(cross_ref, weights_ref, out_ref):
    k = weights_ref.shape[0]
    left = cross_ref[0].reshape(8 * SRC, k)
    result = jnp.dot(left, weights_ref[...], preferred_element_type=jnp.float32)
    result = result.reshape(8, SRC, LAGS)
    for r in range(8):
        out_ref[:, 0, r, :] = result[r]


def correlate(cross, weights):
    k = weights.shape[0]
    return pl.pallas_call(
        lag_kernel,
        grid=(RX // 8,),
        out_shape=jax.ShapeDtypeStruct((SRC, 1, RX, LAGS), jnp.float32),
        in_specs=[
            pl.BlockSpec((1, 8, SRC, k), lambda i: (i, 0, 0, 0)),
            pl.BlockSpec((k, LAGS), lambda i: (0, 0)),
        ],
        out_specs=pl.BlockSpec((SRC, 1, 8, LAGS), lambda i: (0, 0, i, 0)),
        compiler_params=pltpu.CompilerParams(vmem_limit_bytes=32 * 1024 * 1024),
        cost_estimate=pl.CostEstimate(
            flops=2 * SRC * RX * k * LAGS, bytes_accessed=16 * 1024 * 1024, transcendentals=0
        ),
    )(cross, weights)


def solution(mesh):
    chans, bands = mesh.shape["chan"], mesh.shape["band"]

    def local(spectra, source_block, segment_flags):
        valid = jnp.sum(segment_flags)
        tier = (valid > 16).astype(jnp.int32) + (valid > 24).astype(jnp.int32)
        cross = lax.switch(
            tier,
            [functools.partial(stacked, tiles, chans, bands) for tiles in (2, 3, 4)],
            source_block, segment_flags, spectra,
        )
        return correlate(cross, lag_table(bands, chans))

    return jax.shard_map(
        local,
        mesh=mesh,
        in_specs=(P(None, None, "chan", "band"), P(), P()),
        out_specs=P(None, "band", "chan", None),
        check_vma=False,
    )
```

```python
import functools
import math

import jax
import jax.numpy as jnp
from jax import lax
from jax.experimental import pallas as pl
from jax.experimental.pallas import tpu as pltpu
from jax.sharding import PartitionSpec as P

LAGS = 1024
SEG = 30
SRC = 64
BINS = 16
RX = 32
MESH = pl.DeviceIdType.MESH


def lag_rows(parity, start, count):
    shape = (count, LAGS // 2)
    frequency = 2 * (start + lax.broadcasted_iota(jnp.int32, shape, 0)) + parity
    lag = lax.broadcasted_iota(jnp.int32, shape, 1)
    phase = (frequency * (lag + LAGS // 2)) & (LAGS - 1)
    quarter = (phase + LAGS // 8) >> 8
    angle = (phase - (quarter << 8)).astype(jnp.float32) * (2.0 * math.pi / LAGS)
    square = angle * angle
    sine = angle * (1 + square * (-1 / 6 + square * (1 / 120 + square * (-1 / 5040 + square * (1 / 362880)))))
    cosine = 1 + square * (-1 / 2 + square * (1 / 24 + square * (-1 / 720 + square * (1 / 40320))))
    swap = (quarter & 1) == 1
    cos_part = jnp.where(swap, sine, cosine)
    sin_part = jnp.where(swap, cosine, sine)
    weight = jnp.where(frequency == 0, 1.0, 2.0) * (1.0 / math.sqrt(LAGS))
    cos_part = jnp.where(((quarter + 1) & 2) == 2, -cos_part, cos_part) * weight
    sin_part = jnp.where((quarter & 2) == 2, sin_part, -sin_part) * weight
    return cos_part.astype(jnp.bfloat16), sin_part.astype(jnp.bfloat16)


def pack_kernel(tiles, chans, bands, band_ref, block_ref, flags_ref, x_ref, xs_ref, cand_ref, scale_ref, following):
    segs = 8 * tiles
    depth = BINS * segs
    rows = depth // bands
    f32, bf16 = jnp.float32, jnp.bfloat16

    following[SEG] = SEG

    def link(i, valid):
        g = SEG - 1 - i
        following[g] = jnp.where(flags_ref[g] > 0, g, following[g + 1])
        return valid + flags_ref[g]

    valid = lax.fori_loop(0, SEG, link, 0)

    def pack(k, at):
        g = jnp.minimum(at, SEG - 1)
        place = pl.ds(pl.multiple_of(k * BINS, BINS), BINS)
        xs_ref[0, place, :] = x_ref[0, g]
        xs_ref[1, place, :] = x_ref[1, g]
        return following[jnp.minimum(at + 1, SEG)]

    lax.fori_loop(0, segs, pack, following[0])

    first = block_ref[0] * SRC
    width = RX * chans
    owner = first // width
    within = first - owner * width
    lane0 = pl.multiple_of(within // 128 * 128, 128)
    upper = (within // SRC) % 2
    sr = xs_ref[0, :, pl.ds(lane0, 128)].astype(f32)
    si = xs_ref[1, :, pl.ds(lane0, 128)].astype(f32)
    lane = lax.broadcasted_iota(jnp.int32, (depth, 128), 1)
    slot = lax.broadcasted_iota(jnp.int32, (depth, 128), 0) >> 4
    low = jnp.where(lane < SRC, sr, pltpu.roll(si, SRC, 1))
    high = jnp.where(lane < SRC, pltpu.roll(sr, SRC, 1), si)
    mine = jnp.where(upper == 0, low, high)
    count = jnp.where(owner == band_ref[0], valid, 0)
    mine = jnp.where(slot < count, mine, 0.0).astype(bf16)
    cand_ref[...] = mine.reshape(bands, rows, 128)
    scale_ref[...] = 1.0 / jnp.full((8, 128), valid, jnp.int32).astype(f32)


def stack_kernel(
    tiles, chans, bands,
    xs, cand, scale_ref, cross_out, table_out,
    send, recv, parts, zall, spread, cross, turned, table,
    a2a_send, a2a_recv, rs_send, rs_recv, ag_send, ag_recv,
    right_send, right_recv, left_send, left_recv, sib_send, sib_recv, out_sem,
):
    depth = BINS * 8 * tiles
    bins = BINS * chans
    half = chans // 2
    pieces = max(1, half // 4)
    size = half // pieces
    last = bands // 2
    groups = chans // 4
    c = lax.axis_index("chan")
    b = lax.axis_index("band")
    f32, bf16 = jnp.float32, jnp.bfloat16

    barrier = pltpu.get_barrier_semaphore()

    def greet_chan(i, carry):
        pl.semaphore_signal(barrier, inc=1, device_id=(lax.rem(c + i, chans), b), device_id_type=MESH)
        return carry

    def greet_band(i, carry):
        pl.semaphore_signal(barrier, inc=1, device_id=(c, lax.rem(b + i, bands)), device_id_type=MESH)
        return carry

    lax.fori_loop(1, bands, greet_band, 0)
    lax.fori_loop(1, chans, greet_chan, 0)

    def turn(block, carry):
        lanes = pl.ds(pl.multiple_of(block * 128, 128), 128)
        for comp in range(2):
            rows = xs[comp, :, lanes].T
            for q in range(4):
                send[4 * block + q, comp * RX:(comp + 1) * RX, :] = rows[q * RX:(q + 1) * RX]
        return carry

    lax.fori_loop(0, groups, turn, 0)
    recv[c] = send[c]

    pl.semaphore_wait(barrier, chans + bands - 2)

    def rs_copy(other, slot):
        return pltpu.make_async_remote_copy(
            src_ref=cand.at[other], dst_ref=parts.at[slot],
            send_sem=rs_send.at[other], recv_sem=rs_recv.at[slot],
            device_id=(c, other), device_id_type=MESH)

    def rs_start(i, carry):
        rs_copy(lax.rem(b + i, bands), b).start()
        return carry

    lax.fori_loop(1, bands, rs_start, 0)

    count = min(32, bins // 2)

    def fill(i, carry):
        start = pl.multiple_of(i * count, count)
        for parity in range(2):
            cos_part, sin_part = lag_rows(parity, start, count)
            table[parity, pl.ds(start, count), :] = cos_part
            table[parity, pl.ds(bins // 2 + start, count), :] = sin_part
        return carry

    lax.fori_loop(0, bins // 2 // count, fill, 0)
    table_copy = pltpu.make_async_copy(table, table_out, out_sem.at[RX // 8])
    table_copy.start()

    def rs_sum(i, total):
        other = lax.rem(b + i, bands)
        rs_copy(other, other).wait_recv()
        return total + parts[other].astype(f32)

    zall[b, c] = lax.fori_loop(1, bands, rs_sum, cand[b].astype(f32)).astype(bf16)

    def ag_copy(dest, origin):
        return pltpu.make_async_remote_copy(
            src_ref=zall.at[b, origin], dst_ref=zall.at[b, origin],
            send_sem=ag_send.at[dest], recv_sem=ag_recv.at[origin],
            device_id=(dest, b), device_id_type=MESH)

    def ag_start(i, carry):
        ag_copy(lax.rem(c + i, chans), c).start()
        return carry

    lax.fori_loop(1, chans, ag_start, 0)

    def a2a_copy(dest, origin):
        return pltpu.make_async_remote_copy(
            src_ref=send.at[dest], dst_ref=recv.at[origin],
            send_sem=a2a_send.at[dest], recv_sem=a2a_recv.at[origin],
            device_id=(dest, b), device_id_type=MESH)

    def a2a_start(i, carry):
        a2a_copy(lax.rem(c + i, chans), c).start()
        return carry

    lax.fori_loop(1, chans, a2a_start, 0)

    def ag_wait(start, number):
        def one(i, carry):
            @pl.when(start + i != c)
            def _():
                ag_copy(start + i, start + i).wait_recv()
            return carry

        lax.fori_loop(0, number, one, 0)

    core = lax.rem(c, 2)
    twin = c + 1 - 2 * core
    right = lax.rem(b + 1, bands)
    left = lax.rem(b + bands - 1, bands)

    def part(origin, owner, piece, step, way):
        start, number = half * owner + size * piece, size
        if step == last:
            number = size // 2
            if way < 0:
                start = start + number
        return zall.at[origin, pl.ds(start, number)]

    def hop(piece, step, way, which):
        origin = lax.rem(b + bands - way * (step - 1 + which), bands)
        ref = part(origin, core, piece, step, way)
        sems = (right_send, right_recv) if way > 0 else (left_send, left_recv)
        return pltpu.make_async_remote_copy(
            src_ref=ref, dst_ref=ref, send_sem=sems[0].at[piece, step - 1], recv_sem=sems[1].at[piece, step - 1],
            device_id=(c, right if way > 0 else left), device_id_type=MESH)

    def share(piece, step, way, own):
        origin = lax.rem(b + bands - way * step, bands)
        ref = part(origin, core if own else 1 - core, piece, step, way)
        k = 2 * (step - 1) + (0 if way > 0 else 1)
        return pltpu.make_async_remote_copy(
            src_ref=ref, dst_ref=ref, send_sem=sib_send.at[piece, k], recv_sem=sib_recv.at[piece, k],
            device_id=(twin, b), device_id_type=MESH)

    def advance(piece, step):
        if step == 1:
            ag_wait(half * core + size * piece, size)
        else:
            for way in (1, -1):
                hop(piece, step - 1, way, 1).wait_recv()
        if step <= last:
            for way in (1, -1):
                hop(piece, step, way, 0).start()
        if step > 1:
            for way in (1, -1):
                share(piece, step - 1, way, True).start()

    def arrived(piece):
        ag_wait(half * (1 - core) + size * piece, size)
        for step in range(1, last + 1):
            for way in (1, -1):
                share(piece, step, way, False).wait_recv()

    inverse = jnp.broadcast_to(scale_ref[0:1, :], (8 * BINS, 128))
    row = lax.broadcasted_iota(jnp.int32, (BINS, depth), 0)
    row_bin = jnp.where(row < BINS // 2, 2 * row, 2 * row - (BINS - 1))
    kept = row_bin == (lax.broadcasted_iota(jnp.int32, (BINS, depth), 1) & (BINS - 1))
    sign = jnp.where(lax.broadcasted_iota(jnp.int32, (1, 128), 1) < SRC, 1.0, -1.0)

    def stack(j, buffer):
        @pl.when(j != c)
        def _():
            a2a_copy(j, j).wait_recv()
        z = zall[:, j].reshape(depth, 128)
        swapped = (pltpu.roll(z.astype(f32), SRC, 1) * sign).astype(bf16)
        weights = jnp.concatenate([z, swapped], axis=0)
        spread[buffer] = recv[j].astype(f32)
        place = pl.ds(pl.multiple_of(BINS // 2 * j, BINS // 2), BINS // 2)
        for g in range(RX // 8):
            left = []
            for r in range(8 * g, 8 * g + 8):
                line = []
                for comp in range(2):
                    value = jnp.broadcast_to(spread[buffer, comp * RX + r:comp * RX + r + 1, :], (BINS, depth))
                    line.append(jnp.where(kept, value, 0.0).astype(bf16))
                left.append(jnp.concatenate(line, axis=1))
            product = jnp.dot(jnp.concatenate(left, axis=0), weights, preferred_element_type=f32) * inverse
            product = product.reshape(8, BINS, 128)
            cross[0, 8 * g:8 * g + 8, place, :] = product[:, :BINS // 2]
            cross[1, 8 * g:8 * g + 8, place, :] = product[:, BINS // 2:]

    def stack_piece(owner, piece):
        def pair(i, carry):
            for k in range(2):
                stack(half * owner + size * piece + 2 * i + k, k)
            return carry

        lax.fori_loop(0, size // 2, pair, 0)

    first = list(range((pieces + 1) // 2))
    second = list(range((pieces + 1) // 2, pieces))
    for step in range(1, last + 1):
        for piece in first:
            advance(piece, step)
    for piece in second:
        advance(piece, 1)
    for piece in first:
        advance(piece, last + 1)
    for piece in first:
        arrived(piece)
    work = [(owner, piece) for piece in first for owner in range(2)]
    for step in range(2, last + 2):
        if work and second:
            stack_piece(*work.pop(0))
        for piece in second:
            advance(piece, step)
    for piece in second:
        arrived(piece)
    for owner, piece in work + [(owner, piece) for piece in second for owner in range(2)]:
        stack_piece(owner, piece)

    def out_copy(g):
        return pltpu.make_async_copy(turned.at[g], cross_out.at[g], out_sem.at[g])

    k = bins // 2
    for g in range(RX // 8):
        def turn_back(i, carry, g=g):
            for r in (2 * i, 2 * i + 1):
                for parity in range(2):
                    flat = cross[parity, 8 * g + r].astype(bf16).T
                    turned[g, r, :, 2 * parity * k:(2 * parity + 1) * k] = flat[:SRC]
                    turned[g, r, :, (2 * parity + 1) * k:(2 * parity + 2) * k] = flat[SRC:]
            return carry

        lax.fori_loop(0, 4, turn_back, 0)
        out_copy(g).start()

    def rs_done(i, carry):
        rs_copy(lax.rem(b + i, bands), b).wait_send()
        return carry

    def chan_done(i, carry):
        other = lax.rem(c + i, chans)
        a2a_copy(other, c).wait_send()
        ag_copy(other, c).wait_send()
        return carry

    lax.fori_loop(1, bands, rs_done, 0)
    lax.fori_loop(1, chans, chan_done, 0)
    for piece in range(pieces):
        for step in range(1, last + 1):
            for way in (1, -1):
                hop(piece, step, way, 0).wait_send()
                share(piece, step, way, True).wait_send()
    table_copy.wait()
    for g in range(RX // 8):
        out_copy(g).wait()


def stacked(tiles, chans, bands, block, flags, x):
    depth = BINS * 8 * tiles
    rows = depth // bands
    bins = BINS * chans
    pieces = max(1, chans // 8)
    last = bands // 2
    dma = pltpu.SemaphoreType.DMA
    f32, bf16 = jnp.float32, jnp.bfloat16
    vmem = pl.BlockSpec(memory_space=pltpu.VMEM)
    smem = pl.BlockSpec(memory_space=pltpu.SMEM)
    hbm = pl.BlockSpec(memory_space=pl.ANY)
    packed = pl.pallas_call(
        functools.partial(pack_kernel, tiles, chans, bands),
        out_shape=(
            jax.ShapeDtypeStruct((2, depth, RX * chans), bf16),
            jax.ShapeDtypeStruct((bands, rows, 128), bf16),
            jax.ShapeDtypeStruct((8, 128), f32),
        ),
        in_specs=[smem, smem, smem, vmem],
        out_specs=(vmem, vmem, vmem),
        scratch_shapes=[pltpu.SMEM((32,), jnp.int32)],
        compiler_params=pltpu.CompilerParams(vmem_limit_bytes=24 * 1024 * 1024),
    )(lax.axis_index("band").reshape(1), block, flags, x)
    flops = 2 * chans * RX * BINS * 2 * depth * 128
    return pl.pallas_call(
        functools.partial(stack_kernel, tiles, chans, bands),
        out_shape=(
            jax.ShapeDtypeStruct((RX // 8, 8, SRC, 2 * bins), bf16),
            jax.ShapeDtypeStruct((2, bins, LAGS // 2), bf16),
        ),
        in_specs=[vmem] * 3,
        out_specs=(hbm, hbm),
        scratch_shapes=[
            pltpu.VMEM((chans, 2 * RX, depth), bf16),
            pltpu.VMEM((chans, 2 * RX, depth), bf16),
            pltpu.VMEM((bands, rows, 128), bf16),
            pltpu.VMEM((bands, chans, rows, 128), bf16),
            pltpu.VMEM((2, 2 * RX, depth), f32),
            pltpu.VMEM((2, RX, bins // 2, 128), f32),
            pltpu.VMEM((RX // 8, 8, SRC, 2 * bins), bf16),
            pltpu.VMEM((2, bins, LAGS // 2), bf16),
            dma((chans,)), dma((chans,)), dma((bands,)), dma((bands,)), dma((chans,)), dma((chans,)),
            dma((pieces, last)), dma((pieces, last)), dma((pieces, last)), dma((pieces, last)),
            dma((pieces, 2 * last)), dma((pieces, 2 * last)), dma((RX // 8 + 1,)),
        ],
        compiler_params=pltpu.CompilerParams(
            collective_id=tiles, has_side_effects=True, vmem_limit_bytes=48 * 1024 * 1024
        ),
        cost_estimate=pl.CostEstimate(flops=flops, bytes_accessed=8 * 1024 * 1024, transcendentals=0),
    )(*packed)


def lag_kernel(cross_ref, weights_ref, out_ref):
    k = weights_ref.shape[1]
    left = cross_ref[0].reshape(8 * SRC, 2 * k)
    even = jnp.dot(left[:, :k], weights_ref[0], preferred_element_type=jnp.float32)
    odd = jnp.dot(left[:, k:], weights_ref[1], preferred_element_type=jnp.float32)
    low = (even + odd).reshape(8, SRC, LAGS // 2)
    high = (even - odd).reshape(8, SRC, LAGS // 2)
    for r in range(8):
        out_ref[:, 0, r, :LAGS // 2] = low[r]
        out_ref[:, 0, r, LAGS // 2:] = high[r]


def correlate(cross, weights):
    k = weights.shape[1]
    return pl.pallas_call(
        lag_kernel,
        grid=(RX // 8,),
        out_shape=jax.ShapeDtypeStruct((SRC, 1, RX, LAGS), jnp.float32),
        in_specs=[
            pl.BlockSpec((1, 8, SRC, 2 * k), lambda i: (i, 0, 0, 0)),
            pl.BlockSpec((2, k, LAGS // 2), lambda i: (0, 0, 0)),
        ],
        out_specs=pl.BlockSpec((SRC, 1, 8, LAGS), lambda i: (0, 0, i, 0)),
        compiler_params=pltpu.CompilerParams(vmem_limit_bytes=32 * 1024 * 1024),
        cost_estimate=pl.CostEstimate(
            flops=2 * SRC * RX * k * LAGS, bytes_accessed=16 * 1024 * 1024, transcendentals=0
        ),
    )(cross, weights)


def solution(mesh):
    chans, bands = mesh.shape["chan"], mesh.shape["band"]

    def local(spectra, source_block, segment_flags):
        valid = jnp.sum(segment_flags)
        tier = (valid > 16).astype(jnp.int32) + (valid > 24).astype(jnp.int32)
        cross, weights = lax.switch(
            tier,
            [functools.partial(stacked, tiles, chans, bands) for tiles in (2, 3, 4)],
            source_block, segment_flags, spectra,
        )
        return correlate(cross, weights)

    return jax.shard_map(
        local,
        mesh=mesh,
        in_specs=(P(None, None, "chan", "band"), P(), P()),
        out_specs=P(None, "band", "chan", None),
        check_vma=False,
    )
```

```python
import functools
import math

import jax
import jax.numpy as jnp
from jax import lax
from jax.experimental import pallas as pl
from jax.experimental.pallas import tpu as pltpu
from jax.sharding import PartitionSpec as P

LAGS = 1024
SEG = 30
SRC = 64
BINS = 16
RX = 32
MESH = pl.DeviceIdType.MESH


def lag_rows(parity, start, count):
    shape = (count, LAGS // 2)
    frequency = 2 * (start + lax.broadcasted_iota(jnp.int32, shape, 0)) + parity
    lag = lax.broadcasted_iota(jnp.int32, shape, 1)
    phase = (frequency * (lag + LAGS // 2)) & (LAGS - 1)
    quarter = (phase + LAGS // 8) >> 8
    angle = (phase - (quarter << 8)).astype(jnp.float32) * (2.0 * math.pi / LAGS)
    square = angle * angle
    sine = angle * (1 + square * (-1 / 6 + square * (1 / 120 + square * (-1 / 5040 + square * (1 / 362880)))))
    cosine = 1 + square * (-1 / 2 + square * (1 / 24 + square * (-1 / 720 + square * (1 / 40320))))
    swap = (quarter & 1) == 1
    cos_part = jnp.where(swap, sine, cosine)
    sin_part = jnp.where(swap, cosine, sine)
    weight = jnp.where(frequency == 0, 1.0, 2.0) * (1.0 / math.sqrt(LAGS))
    cos_part = jnp.where(((quarter + 1) & 2) == 2, -cos_part, cos_part) * weight
    sin_part = jnp.where((quarter & 2) == 2, sin_part, -sin_part) * weight
    return cos_part.astype(jnp.bfloat16), sin_part.astype(jnp.bfloat16)


def pack_kernel(tiles, chans, bands, band_ref, block_ref, flags_ref, x_ref, xs_ref, cand_ref, scale_ref, following):
    segs = 8 * tiles
    depth = BINS * segs
    rows = depth // bands
    f32, bf16 = jnp.float32, jnp.bfloat16

    following[SEG] = SEG

    def link(i, valid):
        g = SEG - 1 - i
        following[g] = jnp.where(flags_ref[g] > 0, g, following[g + 1])
        return valid + flags_ref[g]

    valid = lax.fori_loop(0, SEG, link, 0)

    def pack(k, at):
        g = jnp.minimum(at, SEG - 1)
        place = pl.ds(pl.multiple_of(k * BINS, BINS), BINS)
        xs_ref[0, place, :] = x_ref[0, g]
        xs_ref[1, place, :] = x_ref[1, g]
        return following[jnp.minimum(at + 1, SEG)]

    lax.fori_loop(0, segs, pack, following[0])

    first = block_ref[0] * SRC
    width = RX * chans
    owner = first // width
    within = first - owner * width
    lane0 = pl.multiple_of(within // 128 * 128, 128)
    upper = (within // SRC) % 2
    sr = xs_ref[0, :, pl.ds(lane0, 128)].astype(f32)
    si = xs_ref[1, :, pl.ds(lane0, 128)].astype(f32)
    lane = lax.broadcasted_iota(jnp.int32, (depth, 128), 1)
    slot = lax.broadcasted_iota(jnp.int32, (depth, 128), 0) >> 4
    low = jnp.where(lane < SRC, sr, pltpu.roll(si, SRC, 1))
    high = jnp.where(lane < SRC, pltpu.roll(sr, SRC, 1), si)
    mine = jnp.where(upper == 0, low, high)
    count = jnp.where(owner == band_ref[0], valid, 0)
    mine = jnp.where(slot < count, mine, 0.0).astype(bf16)
    cand_ref[...] = mine.reshape(bands, rows, 128)
    scale_ref[...] = 1.0 / jnp.full((8, 128), valid, jnp.int32).astype(f32)


def stack_kernel(
    tiles, chans, bands,
    xs, cand, scale_ref, cross_out, table_out,
    send, recv, parts, own, zall, spread, cross, turned, table,
    a2a_send, a2a_recv, rs_send, rs_recv, ag_send, ag_recv,
    right_send, right_recv, left_send, left_recv, sib_send, sib_recv, out_sem,
):
    depth = BINS * 8 * tiles
    bins = BINS * chans
    half = chans // 2
    pieces = max(1, half // 4)
    size = half // pieces
    last = bands // 2
    groups = chans // 4
    c = lax.axis_index("chan")
    b = lax.axis_index("band")
    f32, bf16 = jnp.float32, jnp.bfloat16

    barrier = pltpu.get_barrier_semaphore()

    def greet_chan(i, carry):
        pl.semaphore_signal(barrier, inc=1, device_id=(lax.rem(c + i, chans), b), device_id_type=MESH)
        return carry

    def greet_band(i, carry):
        pl.semaphore_signal(barrier, inc=1, device_id=(c, lax.rem(b + i, bands)), device_id_type=MESH)
        return carry

    lax.fori_loop(1, bands, greet_band, 0)
    lax.fori_loop(1, chans, greet_chan, 0)

    def turn(block, carry):
        lanes = pl.ds(pl.multiple_of(block * 128, 128), 128)
        for comp in range(2):
            rows = xs[comp, :, lanes].T
            for q in range(4):
                send[4 * block + q, comp * RX:(comp + 1) * RX, :] = rows[q * RX:(q + 1) * RX]
        return carry

    lax.fori_loop(0, groups, turn, 0)
    recv[c] = send[c]

    pl.semaphore_wait(barrier, chans + bands - 2)

    def rs_copy(other, slot):
        return pltpu.make_async_remote_copy(
            src_ref=cand.at[other], dst_ref=parts.at[slot],
            send_sem=rs_send.at[other], recv_sem=rs_recv.at[slot],
            device_id=(c, other), device_id_type=MESH)

    def rs_start(i, carry):
        rs_copy(lax.rem(b + i, bands), b).start()
        return carry

    lax.fori_loop(1, bands, rs_start, 0)

    count = min(32, bins // 2)

    def fill(i, carry):
        start = pl.multiple_of(i * count, count)
        for parity in range(2):
            cos_part, sin_part = lag_rows(parity, start, count)
            table[parity, pl.ds(start, count), :] = cos_part
            table[parity, pl.ds(bins // 2 + start, count), :] = sin_part
        return carry

    lax.fori_loop(0, bins // 2 // count, fill, 0)
    table_copy = pltpu.make_async_copy(table, table_out, out_sem.at[RX // 8])
    table_copy.start()

    def rs_sum(i, total):
        other = lax.rem(b + i, bands)
        rs_copy(other, other).wait_recv()
        return total + parts[other].astype(f32)

    core = lax.rem(c, 2)
    twin = c + 1 - 2 * core
    holder = c // half
    own[...] = lax.fori_loop(1, bands, rs_sum, cand[b].astype(f32)).astype(bf16)

    @pl.when(holder == core)
    def _():
        zall[b, c] = own[...]

    def ag_copy(dest, origin):
        return pltpu.make_async_remote_copy(
            src_ref=own, dst_ref=zall.at[b, origin],
            send_sem=ag_send.at[dest // 2], recv_sem=ag_recv.at[origin],
            device_id=(dest, b), device_id_type=MESH)

    def ag_dest(i):
        return 2 * lax.rem(c // 2 + i, half) + holder

    def ag_start(i, carry):
        dest = ag_dest(i)

        @pl.when(dest != c)
        def _():
            ag_copy(dest, c).start()
        return carry

    lax.fori_loop(0, half, ag_start, 0)

    def a2a_copy(dest, origin):
        return pltpu.make_async_remote_copy(
            src_ref=send.at[dest], dst_ref=recv.at[origin],
            send_sem=a2a_send.at[dest], recv_sem=a2a_recv.at[origin],
            device_id=(dest, b), device_id_type=MESH)

    def a2a_start(i, carry):
        a2a_copy(lax.rem(c + i, chans), c).start()
        return carry

    lax.fori_loop(1, chans, a2a_start, 0)

    def ag_wait(start, number):
        def one(i, carry):
            @pl.when(start + i != c)
            def _():
                ag_copy(start + i, start + i).wait_recv()
            return carry

        lax.fori_loop(0, number, one, 0)

    right = lax.rem(b + 1, bands)
    left = lax.rem(b + bands - 1, bands)

    def part(origin, owner, piece, step, way):
        start, number = half * owner + size * piece, size
        if step == last:
            number = size // 2
            if way < 0:
                start = start + number
        return zall.at[origin, pl.ds(start, number)]

    def hop(piece, step, way, which):
        origin = lax.rem(b + bands - way * (step - 1 + which), bands)
        ref = part(origin, core, piece, step, way)
        sems = (right_send, right_recv) if way > 0 else (left_send, left_recv)
        return pltpu.make_async_remote_copy(
            src_ref=ref, dst_ref=ref, send_sem=sems[0].at[piece, step - 1], recv_sem=sems[1].at[piece, step - 1],
            device_id=(c, right if way > 0 else left), device_id_type=MESH)

    def share(piece, step, way, mine):
        origin = lax.rem(b + bands - way * step, bands)
        ref = part(origin, core if mine else 1 - core, piece, step, way)
        k = 2 * step - (1 if way > 0 else 0) if step else 0
        return pltpu.make_async_remote_copy(
            src_ref=ref, dst_ref=ref, send_sem=sib_send.at[piece, k], recv_sem=sib_recv.at[piece, k],
            device_id=(twin, b), device_id_type=MESH)

    def begin(piece):
        ag_wait(half * core + size * piece, size)
        for way in (1, -1):
            hop(piece, 1, way, 0).start()
        share(piece, 0, 1, True).start()

    def advance(piece, step):
        for way in (1, -1):
            hop(piece, step - 1, way, 1).wait_recv()
            if step <= last:
                hop(piece, step, way, 0).start()
            share(piece, step - 1, way, True).start()

    def arrived(piece):
        share(piece, 0, 1, False).wait_recv()
        for step in range(1, last + 1):
            for way in (1, -1):
                share(piece, step, way, False).wait_recv()

    inverse = jnp.broadcast_to(scale_ref[0:1, :], (8 * BINS, 128))
    row = lax.broadcasted_iota(jnp.int32, (BINS, depth), 0)
    row_bin = jnp.where(row < BINS // 2, 2 * row, 2 * row - (BINS - 1))
    kept = row_bin == (lax.broadcasted_iota(jnp.int32, (BINS, depth), 1) & (BINS - 1))
    sign = jnp.where(lax.broadcasted_iota(jnp.int32, (1, 128), 1) < SRC, 1.0, -1.0)

    def stack(j, buffer):
        @pl.when(j != c)
        def _():
            a2a_copy(j, j).wait_recv()
        z = zall[:, j].reshape(depth, 128)
        swapped = (pltpu.roll(z.astype(f32), SRC, 1) * sign).astype(bf16)
        weights = jnp.concatenate([z, swapped], axis=0)
        spread[buffer] = recv[j].astype(f32)
        place = pl.ds(pl.multiple_of(BINS // 2 * j, BINS // 2), BINS // 2)
        for g in range(RX // 8):
            left = []
            for r in range(8 * g, 8 * g + 8):
                line = []
                for comp in range(2):
                    value = jnp.broadcast_to(spread[buffer, comp * RX + r:comp * RX + r + 1, :], (BINS, depth))
                    line.append(jnp.where(kept, value, 0.0).astype(bf16))
                left.append(jnp.concatenate(line, axis=1))
            product = jnp.dot(jnp.concatenate(left, axis=0), weights, preferred_element_type=f32) * inverse
            product = product.reshape(8, BINS, 128)
            cross[0, 8 * g:8 * g + 8, place, :] = product[:, :BINS // 2]
            cross[1, 8 * g:8 * g + 8, place, :] = product[:, BINS // 2:]

    def stack_piece(owner, piece):
        def pair(i, carry):
            for k in range(2):
                stack(half * owner + size * piece + 2 * i + k, k)
            return carry

        lax.fori_loop(0, size // 2, pair, 0)

    for piece in range(pieces):
        begin(piece)
    for step in range(2, last + 2):
        for piece in range(pieces):
            advance(piece, step)
    for piece in range(pieces):
        arrived(piece)
        for owner in range(2):
            stack_piece(owner, piece)

    def out_copy(g):
        return pltpu.make_async_copy(turned.at[g], cross_out.at[g], out_sem.at[g])

    k = bins // 2
    for g in range(RX // 8):
        def turn_back(i, carry, g=g):
            for r in (2 * i, 2 * i + 1):
                for parity in range(2):
                    flat = cross[parity, 8 * g + r].astype(bf16).T
                    turned[g, r, :, 2 * parity * k:(2 * parity + 1) * k] = flat[:SRC]
                    turned[g, r, :, (2 * parity + 1) * k:(2 * parity + 2) * k] = flat[SRC:]
            return carry

        lax.fori_loop(0, 4, turn_back, 0)
        out_copy(g).start()

    def rs_done(i, carry):
        rs_copy(lax.rem(b + i, bands), b).wait_send()
        return carry

    def chan_done(i, carry):
        other = lax.rem(c + i, chans)
        a2a_copy(other, c).wait_send()
        return carry

    def ag_done(i, carry):
        dest = ag_dest(i)

        @pl.when(dest != c)
        def _():
            ag_copy(dest, c).wait_send()
        return carry

    lax.fori_loop(1, bands, rs_done, 0)
    lax.fori_loop(1, chans, chan_done, 0)
    lax.fori_loop(0, half, ag_done, 0)
    for piece in range(pieces):
        share(piece, 0, 1, True).wait_send()
        for step in range(1, last + 1):
            for way in (1, -1):
                hop(piece, step, way, 0).wait_send()
                share(piece, step, way, True).wait_send()
    table_copy.wait()
    for g in range(RX // 8):
        out_copy(g).wait()


def stacked(tiles, chans, bands, block, flags, x):
    depth = BINS * 8 * tiles
    rows = depth // bands
    bins = BINS * chans
    pieces = max(1, chans // 8)
    last = bands // 2
    dma = pltpu.SemaphoreType.DMA
    f32, bf16 = jnp.float32, jnp.bfloat16
    vmem = pl.BlockSpec(memory_space=pltpu.VMEM)
    smem = pl.BlockSpec(memory_space=pltpu.SMEM)
    hbm = pl.BlockSpec(memory_space=pl.ANY)
    packed = pl.pallas_call(
        functools.partial(pack_kernel, tiles, chans, bands),
        out_shape=(
            jax.ShapeDtypeStruct((2, depth, RX * chans), bf16),
            jax.ShapeDtypeStruct((bands, rows, 128), bf16),
            jax.ShapeDtypeStruct((8, 128), f32),
        ),
        in_specs=[smem, smem, smem, vmem],
        out_specs=(vmem, vmem, vmem),
        scratch_shapes=[pltpu.SMEM((32,), jnp.int32)],
        compiler_params=pltpu.CompilerParams(vmem_limit_bytes=24 * 1024 * 1024),
    )(lax.axis_index("band").reshape(1), block, flags, x)
    flops = 2 * chans * RX * BINS * 2 * depth * 128
    return pl.pallas_call(
        functools.partial(stack_kernel, tiles, chans, bands),
        out_shape=(
            jax.ShapeDtypeStruct((RX // 8, 8, SRC, 2 * bins), bf16),
            jax.ShapeDtypeStruct((2, bins, LAGS // 2), bf16),
        ),
        in_specs=[vmem] * 3,
        out_specs=(hbm, hbm),
        scratch_shapes=[
            pltpu.VMEM((chans, 2 * RX, depth), bf16),
            pltpu.VMEM((chans, 2 * RX, depth), bf16),
            pltpu.VMEM((bands, rows, 128), bf16),
            pltpu.VMEM((rows, 128), bf16),
            pltpu.VMEM((bands, chans, rows, 128), bf16),
            pltpu.VMEM((2, 2 * RX, depth), f32),
            pltpu.VMEM((2, RX, bins // 2, 128), f32),
            pltpu.VMEM((RX // 8, 8, SRC, 2 * bins), bf16),
            pltpu.VMEM((2, bins, LAGS // 2), bf16),
            dma((chans,)), dma((chans,)), dma((bands,)), dma((bands,)), dma((chans // 2,)), dma((chans,)),
            dma((pieces, last)), dma((pieces, last)), dma((pieces, last)), dma((pieces, last)),
            dma((pieces, 2 * last + 1)), dma((pieces, 2 * last + 1)), dma((RX // 8 + 1,)),
        ],
        compiler_params=pltpu.CompilerParams(
            collective_id=tiles, has_side_effects=True, vmem_limit_bytes=48 * 1024 * 1024
        ),
        cost_estimate=pl.CostEstimate(flops=flops, bytes_accessed=8 * 1024 * 1024, transcendentals=0),
    )(*packed)


def lag_kernel(cross_ref, weights_ref, out_ref):
    k = weights_ref.shape[1]
    left = cross_ref[0].reshape(8 * SRC, 2 * k)
    even = jnp.dot(left[:, :k], weights_ref[0], preferred_element_type=jnp.float32)
    odd = jnp.dot(left[:, k:], weights_ref[1], preferred_element_type=jnp.float32)
    low = (even + odd).reshape(8, SRC, LAGS // 2)
    high = (even - odd).reshape(8, SRC, LAGS // 2)
    for r in range(8):
        out_ref[:, 0, r, :LAGS // 2] = low[r]
        out_ref[:, 0, r, LAGS // 2:] = high[r]


def correlate(cross, weights):
    k = weights.shape[1]
    return pl.pallas_call(
        lag_kernel,
        grid=(RX // 8,),
        out_shape=jax.ShapeDtypeStruct((SRC, 1, RX, LAGS), jnp.float32),
        in_specs=[
            pl.BlockSpec((1, 8, SRC, 2 * k), lambda i: (i, 0, 0, 0)),
            pl.BlockSpec((2, k, LAGS // 2), lambda i: (0, 0, 0)),
        ],
        out_specs=pl.BlockSpec((SRC, 1, 8, LAGS), lambda i: (0, 0, i, 0)),
        compiler_params=pltpu.CompilerParams(vmem_limit_bytes=32 * 1024 * 1024),
        cost_estimate=pl.CostEstimate(
            flops=2 * SRC * RX * k * LAGS, bytes_accessed=16 * 1024 * 1024, transcendentals=0
        ),
    )(cross, weights)


def solution(mesh):
    chans, bands = mesh.shape["chan"], mesh.shape["band"]

    def local(spectra, source_block, segment_flags):
        valid = jnp.sum(segment_flags)
        tier = (valid > 16).astype(jnp.int32) + (valid > 24).astype(jnp.int32)
        cross, weights = lax.switch(
            tier,
            [functools.partial(stacked, tiles, chans, bands) for tiles in (2, 3, 4)],
            source_block, segment_flags, spectra,
        )
        return correlate(cross, weights)

    return jax.shard_map(
        local,
        mesh=mesh,
        in_specs=(P(None, None, "chan", "band"), P(), P()),
        out_specs=P(None, "band", "chan", None),
        check_vma=False,
    )
```

```python
import functools
import math

import jax
import jax.numpy as jnp
from jax import lax
from jax.experimental import pallas as pl
from jax.experimental.pallas import tpu as pltpu
from jax.sharding import PartitionSpec as P

LAGS = 1024
SEG = 30
SLOTS = 32
SRC = 64
BINS = 16
RX = 32
MESH = pl.DeviceIdType.MESH


def lag_rows(parity, start, count):
    shape = (count, LAGS // 2)
    frequency = 2 * (start + lax.broadcasted_iota(jnp.int32, shape, 0)) + parity
    lag = lax.broadcasted_iota(jnp.int32, shape, 1)
    phase = (frequency * (lag + LAGS // 2)) & (LAGS - 1)
    quarter = (phase + LAGS // 8) >> 8
    angle = (phase - (quarter << 8)).astype(jnp.float32) * (2.0 * math.pi / LAGS)
    square = angle * angle
    sine = angle * (1 + square * (-1 / 6 + square * (1 / 120 + square * (-1 / 5040 + square * (1 / 362880)))))
    cosine = 1 + square * (-1 / 2 + square * (1 / 24 + square * (-1 / 720 + square * (1 / 40320))))
    swap = (quarter & 1) == 1
    cos_part = jnp.where(swap, sine, cosine)
    sin_part = jnp.where(swap, cosine, sine)
    weight = jnp.where(frequency == 0, 1.0, 2.0) * (1.0 / math.sqrt(LAGS))
    cos_part = jnp.where(((quarter + 1) & 2) == 2, -cos_part, cos_part) * weight
    sin_part = jnp.where((quarter & 2) == 2, sin_part, -sin_part) * weight
    return cos_part.astype(jnp.bfloat16), sin_part.astype(jnp.bfloat16)


def pack_kernel(chans, band_ref, block_ref, flags_ref, x_ref, xs_ref, cand_ref, scale_ref, tier_ref, following):
    depth = BINS * SLOTS
    f32, bf16 = jnp.float32, jnp.bfloat16

    following[SEG] = SEG

    def link(i, valid):
        g = SEG - 1 - i
        following[g] = jnp.where(flags_ref[g] > 0, g, following[g + 1])
        return valid + flags_ref[g]

    valid = lax.fori_loop(0, SEG, link, 0)

    def pack(k, at):
        g = jnp.minimum(at, SEG - 1)
        place = pl.ds(pl.multiple_of(k * BINS, BINS), BINS)
        xs_ref[0, place, :] = x_ref[0, g]
        xs_ref[1, place, :] = x_ref[1, g]
        return following[jnp.minimum(at + 1, SEG)]

    tier = jnp.maximum((valid + 7) // 8 - 2, 0)
    tier_ref[0] = tier
    lax.fori_loop(0, 8 * (tier + 2), pack, following[0])

    first = block_ref[0] * SRC
    width = RX * chans
    owner = first // width
    within = first - owner * width
    lane0 = pl.multiple_of(within // 128 * 128, 128)
    upper = (within // SRC) % 2
    sr = xs_ref[0, :, pl.ds(lane0, 128)].astype(f32)
    si = xs_ref[1, :, pl.ds(lane0, 128)].astype(f32)
    lane = lax.broadcasted_iota(jnp.int32, (depth, 128), 1)
    slot = lax.broadcasted_iota(jnp.int32, (depth, 128), 0) >> 4
    low = jnp.where(lane < SRC, sr, pltpu.roll(si, SRC, 1))
    high = jnp.where(lane < SRC, pltpu.roll(sr, SRC, 1), si)
    mine = jnp.where(upper == 0, low, high)
    count = jnp.where(owner == band_ref[0], valid, 0)
    mine = jnp.where(slot < count, mine, 0.0).astype(bf16)
    cand_ref[...] = mine
    scale_ref[...] = 1.0 / jnp.full((8, 128), valid, jnp.int32).astype(f32)


def stack_kernel(
    tiles, chans, bands,
    xs, cand, scale_ref, turned, table,
    send, recv, parts, own, zall, spread, cross,
    a2a_send, a2a_recv, rs_send, rs_recv, ag_send, ag_recv,
    right_send, right_recv, left_send, left_recv, sib_send, sib_recv,
):
    depth = BINS * 8 * tiles
    rows = depth // bands
    bins = BINS * chans
    half = chans // 2
    pieces = max(1, half // 4)
    size = half // pieces
    last = bands // 2
    groups = chans // 4
    c = lax.axis_index("chan")
    b = lax.axis_index("band")
    f32, bf16 = jnp.float32, jnp.bfloat16

    barrier = pltpu.get_barrier_semaphore()

    def greet_chan(i, carry):
        pl.semaphore_signal(barrier, inc=1, device_id=(lax.rem(c + i, chans), b), device_id_type=MESH)
        return carry

    def greet_band(i, carry):
        pl.semaphore_signal(barrier, inc=1, device_id=(c, lax.rem(b + i, bands)), device_id_type=MESH)
        return carry

    lax.fori_loop(1, bands, greet_band, 0)
    lax.fori_loop(1, chans, greet_chan, 0)

    def turn(block, carry):
        lanes = pl.ds(pl.multiple_of(block * 128, 128), 128)
        for comp in range(2):
            lines = xs[comp, :depth, lanes].T
            for q in range(4):
                send[4 * block + q, comp * RX:(comp + 1) * RX, :] = lines[q * RX:(q + 1) * RX]
        return carry

    lax.fori_loop(0, groups, turn, 0)
    recv[c] = send[c]

    pl.semaphore_wait(barrier, chans + bands - 2)

    def rs_copy(other, slot):
        return pltpu.make_async_remote_copy(
            src_ref=cand.at[pl.ds(pl.multiple_of(other * rows, rows), rows)], dst_ref=parts.at[slot],
            send_sem=rs_send.at[other], recv_sem=rs_recv.at[slot],
            device_id=(c, other), device_id_type=MESH)

    def rs_start(i, carry):
        rs_copy(lax.rem(b + i, bands), b).start()
        return carry

    lax.fori_loop(1, bands, rs_start, 0)

    count = min(32, bins // 2)

    def fill(i, carry):
        start = pl.multiple_of(i * count, count)
        for parity in range(2):
            cos_part, sin_part = lag_rows(parity, start, count)
            table[parity, pl.ds(start, count), :] = cos_part
            table[parity, pl.ds(bins // 2 + start, count), :] = sin_part
        return carry

    lax.fori_loop(0, bins // 2 // count, fill, 0)

    def rs_sum(i, total):
        other = lax.rem(b + i, bands)
        rs_copy(other, other).wait_recv()
        return total + parts[other].astype(f32)

    core = lax.rem(c, 2)
    twin = c + 1 - 2 * core
    holder = c // half
    own[...] = lax.fori_loop(1, bands, rs_sum, cand[pl.ds(pl.multiple_of(b * rows, rows), rows), :].astype(f32)).astype(bf16)

    @pl.when(holder == core)
    def _():
        zall[b, c] = own[...]

    def ag_copy(dest, origin):
        return pltpu.make_async_remote_copy(
            src_ref=own, dst_ref=zall.at[b, origin],
            send_sem=ag_send.at[dest // 2], recv_sem=ag_recv.at[origin],
            device_id=(dest, b), device_id_type=MESH)

    def ag_dest(i):
        return 2 * lax.rem(c // 2 + i, half) + holder

    def ag_start(i, carry):
        dest = ag_dest(i)

        @pl.when(dest != c)
        def _():
            ag_copy(dest, c).start()
        return carry

    lax.fori_loop(0, half, ag_start, 0)

    def a2a_copy(dest, origin):
        return pltpu.make_async_remote_copy(
            src_ref=send.at[dest], dst_ref=recv.at[origin],
            send_sem=a2a_send.at[dest], recv_sem=a2a_recv.at[origin],
            device_id=(dest, b), device_id_type=MESH)

    def a2a_start(i, carry):
        a2a_copy(lax.rem(c + i, chans), c).start()
        return carry

    lax.fori_loop(1, chans, a2a_start, 0)

    def ag_wait(start, number):
        def one(i, carry):
            @pl.when(start + i != c)
            def _():
                ag_copy(start + i, start + i).wait_recv()
            return carry

        lax.fori_loop(0, number, one, 0)

    right = lax.rem(b + 1, bands)
    left = lax.rem(b + bands - 1, bands)

    def part(origin, owner, piece, step, way):
        start, number = half * owner + size * piece, size
        if step == last:
            number = size // 2
            if way < 0:
                start = start + number
        return zall.at[origin, pl.ds(start, number)]

    def hop(piece, step, way, which):
        origin = lax.rem(b + bands - way * (step - 1 + which), bands)
        ref = part(origin, core, piece, step, way)
        sems = (right_send, right_recv) if way > 0 else (left_send, left_recv)
        return pltpu.make_async_remote_copy(
            src_ref=ref, dst_ref=ref, send_sem=sems[0].at[piece, step - 1], recv_sem=sems[1].at[piece, step - 1],
            device_id=(c, right if way > 0 else left), device_id_type=MESH)

    def share(piece, step, way, mine):
        origin = lax.rem(b + bands - way * step, bands)
        ref = part(origin, core if mine else 1 - core, piece, step, way)
        k = 2 * step - (1 if way > 0 else 0) if step else 0
        return pltpu.make_async_remote_copy(
            src_ref=ref, dst_ref=ref, send_sem=sib_send.at[piece, k], recv_sem=sib_recv.at[piece, k],
            device_id=(twin, b), device_id_type=MESH)

    def begin(piece):
        ag_wait(half * core + size * piece, size)
        for way in (1, -1):
            hop(piece, 1, way, 0).start()
        share(piece, 0, 1, True).start()

    def advance(piece, step):
        for way in (1, -1):
            hop(piece, step - 1, way, 1).wait_recv()
            if step <= last:
                hop(piece, step, way, 0).start()
            share(piece, step - 1, way, True).start()

    def arrived(piece):
        share(piece, 0, 1, False).wait_recv()
        for step in range(1, last + 1):
            for way in (1, -1):
                share(piece, step, way, False).wait_recv()

    inverse = jnp.broadcast_to(scale_ref[0:1, :], (8 * BINS, 128))
    row = lax.broadcasted_iota(jnp.int32, (BINS, depth), 0)
    row_bin = jnp.where(row < BINS // 2, 2 * row, 2 * row - (BINS - 1))
    kept = row_bin == (lax.broadcasted_iota(jnp.int32, (BINS, depth), 1) & (BINS - 1))
    sign = jnp.where(lax.broadcasted_iota(jnp.int32, (1, 128), 1) < SRC, 1.0, -1.0)

    def stack(j, buffer):
        z = zall[:, j].reshape(depth, 128)
        swapped = (pltpu.roll(z.astype(f32), SRC, 1) * sign).astype(bf16)
        weights = jnp.concatenate([z, swapped], axis=0)
        spread[buffer] = recv[j].astype(f32)
        place = pl.ds(pl.multiple_of(BINS // 2 * j, BINS // 2), BINS // 2)
        for g in range(RX // 8):
            left = []
            for r in range(8 * g, 8 * g + 8):
                line = []
                for comp in range(2):
                    value = jnp.broadcast_to(spread[buffer, comp * RX + r:comp * RX + r + 1, :], (BINS, depth))
                    line.append(jnp.where(kept, value, 0.0).astype(bf16))
                left.append(jnp.concatenate(line, axis=1))
            product = jnp.dot(jnp.concatenate(left, axis=0), weights, preferred_element_type=f32) * inverse
            product = product.reshape(8, BINS, 128)
            cross[0, 8 * g:8 * g + 8, place, :] = product[:, :BINS // 2]
            cross[1, 8 * g:8 * g + 8, place, :] = product[:, BINS // 2:]

    def stack_piece(owner, piece):
        start = half * owner + size * piece

        def a2a_wait(i, carry):
            @pl.when(start + i != c)
            def _():
                a2a_copy(start + i, start + i).wait_recv()
            return carry

        lax.fori_loop(0, size, a2a_wait, 0)
        for k in range(size):
            stack(start + k, k)

    def finish(piece):
        arrived(piece)

        def both(owner, carry):
            stack_piece(owner, piece)
            return carry

        lax.fori_loop(0, 2, both, 0)

    for piece in range(pieces):
        begin(piece)
    if pieces == 4 and last == 4:
        order = [(0, 2), (1, 2), (2, 2), (0, 3), (1, 3), (3, 2), (0, 4), (1, 4), (2, 3), (3, 3), (0, 5), (1, 5), (2, 4), (3, 4)]
        for piece, step in order:
            advance(piece, step)
        finish(0)
        advance(2, 5)
        advance(3, 5)
        for piece in range(1, pieces):
            finish(piece)
    else:
        for step in range(2, last + 2):
            for piece in range(pieces):
                advance(piece, step)
        for piece in range(pieces):
            finish(piece)

    k = bins // 2
    for g in range(RX // 8):
        def turn_back(i, carry, g=g):
            for r in (2 * i, 2 * i + 1):
                for parity in range(2):
                    flat = cross[parity, 8 * g + r].astype(bf16).T
                    turned[8 * g + r, :, 2 * parity * k:(2 * parity + 1) * k] = flat[:SRC]
                    turned[8 * g + r, :, (2 * parity + 1) * k:(2 * parity + 2) * k] = flat[SRC:]
            return carry

        lax.fori_loop(0, 4, turn_back, 0)

    def rs_done(i, carry):
        rs_copy(lax.rem(b + i, bands), b).wait_send()
        return carry

    def chan_done(i, carry):
        other = lax.rem(c + i, chans)
        a2a_copy(other, c).wait_send()
        return carry

    def ag_done(i, carry):
        dest = ag_dest(i)

        @pl.when(dest != c)
        def _():
            ag_copy(dest, c).wait_send()
        return carry

    lax.fori_loop(1, bands, rs_done, 0)
    lax.fori_loop(1, chans, chan_done, 0)
    lax.fori_loop(0, half, ag_done, 0)
    for piece in range(pieces):
        share(piece, 0, 1, True).wait_send()
        for step in range(1, last + 1):
            for way in (1, -1):
                hop(piece, step, way, 0).wait_send()
                share(piece, step, way, True).wait_send()


def packed(chans, block, flags, x):
    vmem = pl.BlockSpec(memory_space=pltpu.VMEM)
    smem = pl.BlockSpec(memory_space=pltpu.SMEM)
    depth = BINS * SLOTS
    return pl.pallas_call(
        functools.partial(pack_kernel, chans),
        out_shape=(
            jax.ShapeDtypeStruct((2, depth, RX * chans), jnp.bfloat16),
            jax.ShapeDtypeStruct((depth, 128), jnp.bfloat16),
            jax.ShapeDtypeStruct((8, 128), jnp.float32),
            jax.ShapeDtypeStruct((1,), jnp.int32),
        ),
        in_specs=[smem, smem, smem, vmem],
        out_specs=(vmem, vmem, vmem, smem),
        scratch_shapes=[pltpu.SMEM((SLOTS,), jnp.int32)],
        compiler_params=pltpu.CompilerParams(vmem_limit_bytes=24 * 1024 * 1024),
    )(lax.axis_index("band").reshape(1), block, flags, x)


def stacked(tiles, chans, bands, xs, cand, scale):
    depth = BINS * 8 * tiles
    rows = depth // bands
    bins = BINS * chans
    pieces = max(1, chans // 8)
    size = chans // 2 // pieces
    last = bands // 2
    dma = pltpu.SemaphoreType.DMA
    f32, bf16 = jnp.float32, jnp.bfloat16
    vmem = pl.BlockSpec(memory_space=pltpu.VMEM)
    flops = 2 * chans * RX * BINS * 2 * depth * 128
    return pl.pallas_call(
        functools.partial(stack_kernel, tiles, chans, bands),
        out_shape=(
            jax.ShapeDtypeStruct((RX, SRC, 2 * bins), bf16),
            jax.ShapeDtypeStruct((2, bins, LAGS // 2), bf16),
        ),
        in_specs=[vmem] * 3,
        out_specs=(vmem, vmem),
        scratch_shapes=[
            pltpu.VMEM((chans, 2 * RX, depth), bf16),
            pltpu.VMEM((chans, 2 * RX, depth), bf16),
            pltpu.VMEM((bands, rows, 128), bf16),
            pltpu.VMEM((rows, 128), bf16),
            pltpu.VMEM((bands, chans, rows, 128), bf16),
            pltpu.VMEM((size, 2 * RX, depth), f32),
            pltpu.VMEM((2, RX, bins // 2, 128), f32),
            dma((chans,)), dma((chans,)), dma((bands,)), dma((bands,)), dma((chans // 2,)), dma((chans,)),
            dma((pieces, last)), dma((pieces, last)), dma((pieces, last)), dma((pieces, last)),
            dma((pieces, 2 * last + 1)), dma((pieces, 2 * last + 1)),
        ],
        compiler_params=pltpu.CompilerParams(
            collective_id=tiles, has_side_effects=True, vmem_limit_bytes=36 * 1024 * 1024
        ),
        cost_estimate=pl.CostEstimate(flops=flops, bytes_accessed=8 * 1024 * 1024, transcendentals=0),
    )(xs, cand, scale)


def lag_kernel(cross_ref, weights_ref, out_ref):
    k = weights_ref.shape[1]
    for q in range(SRC // BINS):
        sources = slice(BINS * q, BINS * q + BINS)
        left = cross_ref[:, sources, :].reshape(RX * BINS, 2 * k)
        even = jnp.dot(left[:, :k], weights_ref[0], preferred_element_type=jnp.float32)
        odd = jnp.dot(left[:, k:], weights_ref[1], preferred_element_type=jnp.float32)
        low = (even + odd).reshape(RX, BINS, LAGS // 2)
        high = (even - odd).reshape(RX, BINS, LAGS // 2)
        for r in range(RX):
            out_ref[sources, 0, r, :LAGS // 2] = low[r]
            out_ref[sources, 0, r, LAGS // 2:] = high[r]


def correlate(cross, weights):
    k = weights.shape[1]
    vmem = pl.BlockSpec(memory_space=pltpu.VMEM)
    return pl.pallas_call(
        lag_kernel,
        out_shape=jax.ShapeDtypeStruct((SRC, 1, RX, LAGS), jnp.float32),
        in_specs=[vmem] * 2,
        out_specs=vmem,
        compiler_params=pltpu.CompilerParams(vmem_limit_bytes=32 * 1024 * 1024),
        cost_estimate=pl.CostEstimate(
            flops=2 * SRC * RX * k * LAGS, bytes_accessed=16 * 1024 * 1024, transcendentals=0
        ),
    )(cross, weights)


def solution(mesh):
    chans, bands = mesh.shape["chan"], mesh.shape["band"]

    def local(spectra, source_block, segment_flags):
        *operands, tier = packed(chans, source_block, segment_flags, spectra)

        def branch(tiles):
            return lambda *arrays: correlate(*stacked(tiles, chans, bands, *arrays))

        return lax.switch(tier[0], [branch(tiles) for tiles in (2, 3, 4)], *operands)

    return jax.shard_map(
        local,
        mesh=mesh,
        in_specs=(P(None, None, "chan", "band"), P(), P()),
        out_specs=P(None, "band", "chan", None),
        check_vma=False,
    )
```

```python
import functools
import math

import jax
import jax.numpy as jnp
from jax import lax
from jax.experimental import pallas as pl
from jax.experimental.pallas import tpu as pltpu
from jax.sharding import PartitionSpec as P

LAGS = 1024
SEG = 30
SLOTS = 32
SRC = 64
BINS = 16
RX = 32
MESH = pl.DeviceIdType.MESH


def lag_rows(parity, start, count):
    shape = (count, LAGS // 2)
    frequency = 2 * (start + lax.broadcasted_iota(jnp.int32, shape, 0)) + parity
    lag = lax.broadcasted_iota(jnp.int32, shape, 1)
    phase = (frequency * (lag + LAGS // 2)) & (LAGS - 1)
    quarter = (phase + LAGS // 8) >> 8
    angle = (phase - (quarter << 8)).astype(jnp.float32) * (2.0 * math.pi / LAGS)
    square = angle * angle
    sine = angle * (1 + square * (-1 / 6 + square * (1 / 120 + square * (-1 / 5040 + square * (1 / 362880)))))
    cosine = 1 + square * (-1 / 2 + square * (1 / 24 + square * (-1 / 720 + square * (1 / 40320))))
    swap = (quarter & 1) == 1
    cos_part = jnp.where(swap, sine, cosine)
    sin_part = jnp.where(swap, cosine, sine)
    weight = jnp.where(frequency == 0, 1.0, 2.0) * (1.0 / math.sqrt(LAGS))
    cos_part = jnp.where(((quarter + 1) & 2) == 2, -cos_part, cos_part) * weight
    sin_part = jnp.where((quarter & 2) == 2, sin_part, -sin_part) * weight
    return cos_part.astype(jnp.bfloat16), sin_part.astype(jnp.bfloat16)


def pack_kernel(chans, band_ref, block_ref, flags_ref, x_ref, xs_ref, cand_ref, scale_ref, tier_ref, following):
    depth = BINS * SLOTS
    f32, bf16 = jnp.float32, jnp.bfloat16

    following[SEG] = SEG

    def link(i, valid):
        g = SEG - 1 - i
        following[g] = jnp.where(flags_ref[g] > 0, g, following[g + 1])
        return valid + flags_ref[g]

    valid = lax.fori_loop(0, SEG, link, 0)

    def pack(k, at):
        g = jnp.minimum(at, SEG - 1)
        place = pl.ds(pl.multiple_of(k * BINS, BINS), BINS)
        xs_ref[0, place, :] = x_ref[0, g]
        xs_ref[1, place, :] = x_ref[1, g]
        return following[jnp.minimum(at + 1, SEG)]

    tier = jnp.maximum((valid + 7) // 8 - 2, 0)
    tier_ref[0] = tier
    lax.fori_loop(0, 8 * (tier + 2), pack, following[0])

    first = block_ref[0] * SRC
    width = RX * chans
    owner = first // width
    within = first - owner * width
    lane0 = pl.multiple_of(within // 128 * 128, 128)
    upper = (within // SRC) % 2
    sr = xs_ref[0, :, pl.ds(lane0, 128)].astype(f32)
    si = xs_ref[1, :, pl.ds(lane0, 128)].astype(f32)
    lane = lax.broadcasted_iota(jnp.int32, (depth, 128), 1)
    slot = lax.broadcasted_iota(jnp.int32, (depth, 128), 0) >> 4
    low = jnp.where(lane < SRC, sr, pltpu.roll(si, SRC, 1))
    high = jnp.where(lane < SRC, pltpu.roll(sr, SRC, 1), si)
    mine = jnp.where(upper == 0, low, high)
    count = jnp.where(owner == band_ref[0], valid, 0)
    mine = jnp.where(slot < count, mine, 0.0).astype(bf16)
    cand_ref[...] = mine
    scale_ref[...] = 1.0 / jnp.full((8, 128), valid, jnp.int32).astype(f32)


def stack_kernel(
    tiles, chans, bands,
    xs, cand, scale_ref, turned, table,
    send, recv, parts, own, zall, spread, cross,
    a2a_send, a2a_recv, rs_send, rs_recv, ag_send, ag_recv,
    right_send, right_recv, left_send, left_recv, sib_send, sib_recv,
):
    depth = BINS * 8 * tiles
    rows = depth // bands
    bins = BINS * chans
    half = chans // 2
    pieces = max(1, half // 8)
    size = half // pieces
    last = bands // 2
    groups = chans // 4
    c = lax.axis_index("chan")
    b = lax.axis_index("band")
    f32, bf16 = jnp.float32, jnp.bfloat16

    barrier = pltpu.get_barrier_semaphore()

    def greet_chan(i, carry):
        pl.semaphore_signal(barrier, inc=1, device_id=(lax.rem(c + i, chans), b), device_id_type=MESH)
        return carry

    def greet_band(i, carry):
        pl.semaphore_signal(barrier, inc=1, device_id=(c, lax.rem(b + i, bands)), device_id_type=MESH)
        return carry

    lax.fori_loop(1, bands, greet_band, 0)
    lax.fori_loop(1, chans, greet_chan, 0)

    def turn(block, carry):
        lanes = pl.ds(pl.multiple_of(block * 128, 128), 128)
        for comp in range(2):
            lines = xs[comp, :depth, lanes].T
            for q in range(4):
                send[4 * block + q, comp * RX:(comp + 1) * RX, :] = lines[q * RX:(q + 1) * RX]
        return carry

    lax.fori_loop(0, groups, turn, 0)
    recv[c] = send[c]

    pl.semaphore_wait(barrier, chans + bands - 2)

    def rs_copy(other, slot):
        return pltpu.make_async_remote_copy(
            src_ref=cand.at[pl.ds(pl.multiple_of(other * rows, rows), rows)], dst_ref=parts.at[slot],
            send_sem=rs_send.at[other], recv_sem=rs_recv.at[slot],
            device_id=(c, other), device_id_type=MESH)

    def rs_start(i, carry):
        rs_copy(lax.rem(b + i, bands), b).start()
        return carry

    lax.fori_loop(1, bands, rs_start, 0)

    count = min(32, bins // 2)

    def fill(i, carry):
        start = pl.multiple_of(i * count, count)
        for parity in range(2):
            cos_part, sin_part = lag_rows(parity, start, count)
            table[parity, pl.ds(start, count), :] = cos_part
            table[parity, pl.ds(bins // 2 + start, count), :] = sin_part
        return carry

    lax.fori_loop(0, bins // 2 // count, fill, 0)

    def rs_sum(i, total):
        other = lax.rem(b + i, bands)
        rs_copy(other, other).wait_recv()
        return total + parts[other].astype(f32)

    core = lax.rem(c, 2)
    twin = c + 1 - 2 * core
    holder = c // half
    own[...] = lax.fori_loop(1, bands, rs_sum, cand[pl.ds(pl.multiple_of(b * rows, rows), rows), :].astype(f32)).astype(bf16)

    @pl.when(holder == core)
    def _():
        zall[b, c] = own[...]

    def ag_copy(dest, origin):
        return pltpu.make_async_remote_copy(
            src_ref=own, dst_ref=zall.at[b, origin],
            send_sem=ag_send.at[dest // 2], recv_sem=ag_recv.at[origin],
            device_id=(dest, b), device_id_type=MESH)

    def ag_dest(i):
        return 2 * lax.rem(c // 2 + i, half) + holder

    def ag_start(i, carry):
        dest = ag_dest(i)

        @pl.when(dest != c)
        def _():
            ag_copy(dest, c).start()
        return carry

    lax.fori_loop(0, half, ag_start, 0)

    def a2a_copy(dest, origin):
        return pltpu.make_async_remote_copy(
            src_ref=send.at[dest], dst_ref=recv.at[origin],
            send_sem=a2a_send.at[dest], recv_sem=a2a_recv.at[origin],
            device_id=(dest, b), device_id_type=MESH)

    def a2a_start(i, carry):
        a2a_copy(lax.rem(c + i, chans), c).start()
        return carry

    def ag_wait(start, number):
        def one(i, carry):
            @pl.when(start + i != c)
            def _():
                ag_copy(start + i, start + i).wait_recv()
            return carry

        lax.fori_loop(0, number, one, 0)

    right = lax.rem(b + 1, bands)
    left = lax.rem(b + bands - 1, bands)

    def part(origin, owner, piece, step, way):
        start, number = half * owner + size * piece, size
        if step == last:
            number = size // 2
            if way < 0:
                start = start + number
        return zall.at[origin, pl.ds(start, number)]

    def hop(piece, step, way, which):
        origin = lax.rem(b + bands - way * (step - 1 + which), bands)
        ref = part(origin, core, piece, step, way)
        sems = (right_send, right_recv) if way > 0 else (left_send, left_recv)
        return pltpu.make_async_remote_copy(
            src_ref=ref, dst_ref=ref, send_sem=sems[0].at[piece, step - 1], recv_sem=sems[1].at[piece, step - 1],
            device_id=(c, right if way > 0 else left), device_id_type=MESH)

    def share(piece, step, way, mine):
        origin = lax.rem(b + bands - way * step, bands)
        ref = part(origin, core if mine else 1 - core, piece, step, way)
        k = 2 * step - (1 if way > 0 else 0) if step else 0
        return pltpu.make_async_remote_copy(
            src_ref=ref, dst_ref=ref, send_sem=sib_send.at[piece, k], recv_sem=sib_recv.at[piece, k],
            device_id=(twin, b), device_id_type=MESH)

    def begin(piece):
        ag_wait(half * core + size * piece, size)
        for way in (1, -1):
            hop(piece, 1, way, 0).start()
        share(piece, 0, 1, True).start()

    def advance(piece, step):
        for way in (1, -1):
            hop(piece, step - 1, way, 1).wait_recv()
            if step <= last:
                hop(piece, step, way, 0).start()
            share(piece, step - 1, way, True).start()

    def arrived(piece):
        share(piece, 0, 1, False).wait_recv()
        for step in range(1, last + 1):
            for way in (1, -1):
                share(piece, step, way, False).wait_recv()

    inverse = jnp.broadcast_to(scale_ref[0:1, :], (8 * BINS, 128))
    row = lax.broadcasted_iota(jnp.int32, (BINS, depth), 0)
    row_bin = jnp.where(row < BINS // 2, 2 * row, 2 * row - (BINS - 1))
    kept = row_bin == (lax.broadcasted_iota(jnp.int32, (BINS, depth), 1) & (BINS - 1))
    sign = jnp.where(lax.broadcasted_iota(jnp.int32, (1, 128), 1) < SRC, 1.0, -1.0)

    def stack(j, buffer):
        z = zall[:, j].reshape(depth, 128)
        swapped = (pltpu.roll(z.astype(f32), SRC, 1) * sign).astype(bf16)
        weights = jnp.concatenate([z, swapped], axis=0)
        spread[buffer] = recv[j].astype(f32)
        place = pl.ds(pl.multiple_of(BINS // 2 * j, BINS // 2), BINS // 2)
        for g in range(RX // 8):
            left = []
            for r in range(8 * g, 8 * g + 8):
                line = []
                for comp in range(2):
                    value = jnp.broadcast_to(spread[buffer, comp * RX + r:comp * RX + r + 1, :], (BINS, depth))
                    line.append(jnp.where(kept, value, 0.0).astype(bf16))
                left.append(jnp.concatenate(line, axis=1))
            product = jnp.dot(jnp.concatenate(left, axis=0), weights, preferred_element_type=f32) * inverse
            product = product.reshape(8, BINS, 128)
            cross[0, 8 * g:8 * g + 8, place, :] = product[:, :BINS // 2]
            cross[1, 8 * g:8 * g + 8, place, :] = product[:, BINS // 2:]

    def stack_piece(owner, piece):
        few = min(size, 4)

        def group(g, carry):
            start = half * owner + size * piece + few * g

            def a2a_wait(i, inner):
                @pl.when(start + i != c)
                def _():
                    a2a_copy(start + i, start + i).wait_recv()
                return inner

            lax.fori_loop(0, few, a2a_wait, 0)
            for k in range(few):
                stack(start + k, k)
            return carry

        lax.fori_loop(0, size // few, group, 0)

    def finish(piece):
        arrived(piece)

        def both(owner, carry):
            stack_piece(owner, piece)
            return carry

        lax.fori_loop(0, 2, both, 0)

    for piece in range(pieces):
        begin(piece)
    lax.fori_loop(1, chans, a2a_start, 0)
    for step in range(2, last + 2):
        for piece in range(pieces):
            advance(piece, step)
    for piece in range(pieces):
        finish(piece)

    k = bins // 2
    for g in range(RX // 8):
        def turn_back(i, carry, g=g):
            for r in (2 * i, 2 * i + 1):
                for parity in range(2):
                    flat = cross[parity, 8 * g + r].astype(bf16).T
                    turned[8 * g + r, :, 2 * parity * k:(2 * parity + 1) * k] = flat[:SRC]
                    turned[8 * g + r, :, (2 * parity + 1) * k:(2 * parity + 2) * k] = flat[SRC:]
            return carry

        lax.fori_loop(0, 4, turn_back, 0)

    def rs_done(i, carry):
        rs_copy(lax.rem(b + i, bands), b).wait_send()
        return carry

    def chan_done(i, carry):
        other = lax.rem(c + i, chans)
        a2a_copy(other, c).wait_send()
        return carry

    def ag_done(i, carry):
        dest = ag_dest(i)

        @pl.when(dest != c)
        def _():
            ag_copy(dest, c).wait_send()
        return carry

    lax.fori_loop(1, bands, rs_done, 0)
    lax.fori_loop(1, chans, chan_done, 0)
    lax.fori_loop(0, half, ag_done, 0)
    for piece in range(pieces):
        share(piece, 0, 1, True).wait_send()
        for step in range(1, last + 1):
            for way in (1, -1):
                hop(piece, step, way, 0).wait_send()
                share(piece, step, way, True).wait_send()


def packed(chans, block, flags, x):
    vmem = pl.BlockSpec(memory_space=pltpu.VMEM)
    smem = pl.BlockSpec(memory_space=pltpu.SMEM)
    depth = BINS * SLOTS
    return pl.pallas_call(
        functools.partial(pack_kernel, chans),
        out_shape=(
            jax.ShapeDtypeStruct((2, depth, RX * chans), jnp.bfloat16),
            jax.ShapeDtypeStruct((depth, 128), jnp.bfloat16),
            jax.ShapeDtypeStruct((8, 128), jnp.float32),
            jax.ShapeDtypeStruct((1,), jnp.int32),
        ),
        in_specs=[smem, smem, smem, vmem],
        out_specs=(vmem, vmem, vmem, smem),
        scratch_shapes=[pltpu.SMEM((SLOTS,), jnp.int32)],
        compiler_params=pltpu.CompilerParams(vmem_limit_bytes=24 * 1024 * 1024),
    )(lax.axis_index("band").reshape(1), block, flags, x)


def stacked(tiles, chans, bands, xs, cand, scale):
    depth = BINS * 8 * tiles
    rows = depth // bands
    bins = BINS * chans
    pieces = max(1, chans // 16)
    last = bands // 2
    dma = pltpu.SemaphoreType.DMA
    f32, bf16 = jnp.float32, jnp.bfloat16
    vmem = pl.BlockSpec(memory_space=pltpu.VMEM)
    flops = 2 * chans * RX * BINS * 2 * depth * 128
    return pl.pallas_call(
        functools.partial(stack_kernel, tiles, chans, bands),
        out_shape=(
            jax.ShapeDtypeStruct((RX, SRC, 2 * bins), bf16),
            jax.ShapeDtypeStruct((2, bins, LAGS // 2), bf16),
        ),
        in_specs=[vmem] * 3,
        out_specs=(vmem, vmem),
        scratch_shapes=[
            pltpu.VMEM((chans, 2 * RX, depth), bf16),
            pltpu.VMEM((chans, 2 * RX, depth), bf16),
            pltpu.VMEM((bands, rows, 128), bf16),
            pltpu.VMEM((rows, 128), bf16),
            pltpu.VMEM((bands, chans, rows, 128), bf16),
            pltpu.VMEM((4, 2 * RX, depth), f32),
            pltpu.VMEM((2, RX, bins // 2, 128), f32),
            dma((chans,)), dma((chans,)), dma((bands,)), dma((bands,)), dma((chans // 2,)), dma((chans,)),
            dma((pieces, last)), dma((pieces, last)), dma((pieces, last)), dma((pieces, last)),
            dma((pieces, 2 * last + 1)), dma((pieces, 2 * last + 1)),
        ],
        compiler_params=pltpu.CompilerParams(
            collective_id=tiles, has_side_effects=True, vmem_limit_bytes=36 * 1024 * 1024
        ),
        cost_estimate=pl.CostEstimate(flops=flops, bytes_accessed=8 * 1024 * 1024, transcendentals=0),
    )(xs, cand, scale)


def lag_kernel(cross_ref, weights_ref, out_ref):
    k = weights_ref.shape[1]
    for q in range(SRC // BINS):
        sources = slice(BINS * q, BINS * q + BINS)
        left = cross_ref[:, sources, :].reshape(RX * BINS, 2 * k)
        even = jnp.dot(left[:, :k], weights_ref[0], preferred_element_type=jnp.float32)
        odd = jnp.dot(left[:, k:], weights_ref[1], preferred_element_type=jnp.float32)
        low = (even + odd).reshape(RX, BINS, LAGS // 2)
        high = (even - odd).reshape(RX, BINS, LAGS // 2)
        for r in range(RX):
            out_ref[sources, 0, r, :LAGS // 2] = low[r]
            out_ref[sources, 0, r, LAGS // 2:] = high[r]


def correlate(cross, weights):
    k = weights.shape[1]
    vmem = pl.BlockSpec(memory_space=pltpu.VMEM)
    return pl.pallas_call(
        lag_kernel,
        out_shape=jax.ShapeDtypeStruct((SRC, 1, RX, LAGS), jnp.float32),
        in_specs=[vmem] * 2,
        out_specs=vmem,
        compiler_params=pltpu.CompilerParams(vmem_limit_bytes=32 * 1024 * 1024),
        cost_estimate=pl.CostEstimate(
            flops=2 * SRC * RX * k * LAGS, bytes_accessed=16 * 1024 * 1024, transcendentals=0
        ),
    )(cross, weights)


def solution(mesh):
    chans, bands = mesh.shape["chan"], mesh.shape["band"]

    def local(spectra, source_block, segment_flags):
        *operands, tier = packed(chans, source_block, segment_flags, spectra)

        def branch(tiles):
            return lambda *arrays: correlate(*stacked(tiles, chans, bands, *arrays))

        return lax.switch(tier[0], [branch(tiles) for tiles in (2, 3, 4)], *operands)

    return jax.shard_map(
        local,
        mesh=mesh,
        in_specs=(P(None, None, "chan", "band"), P(), P()),
        out_specs=P(None, "band", "chan", None),
        check_vma=False,
    )
```

```python
import functools
import math

import jax
import jax.numpy as jnp
from jax import lax
from jax.experimental import pallas as pl
from jax.experimental.pallas import tpu as pltpu
from jax.sharding import PartitionSpec as P

LAGS = 1024
SEG = 30
SLOTS = 32
SRC = 64
BINS = 16
RX = 32
MESH = pl.DeviceIdType.MESH


def lag_rows(parity, start, count):
    shape = (count, LAGS // 2)
    frequency = 2 * (start + lax.broadcasted_iota(jnp.int32, shape, 0)) + parity
    lag = lax.broadcasted_iota(jnp.int32, shape, 1)
    phase = (frequency * (lag + LAGS // 2)) & (LAGS - 1)
    quarter = (phase + LAGS // 8) >> 8
    angle = (phase - (quarter << 8)).astype(jnp.float32) * (2.0 * math.pi / LAGS)
    square = angle * angle
    sine = angle * (1 + square * (-1 / 6 + square * (1 / 120 + square * (-1 / 5040 + square * (1 / 362880)))))
    cosine = 1 + square * (-1 / 2 + square * (1 / 24 + square * (-1 / 720 + square * (1 / 40320))))
    swap = (quarter & 1) == 1
    cos_part = jnp.where(swap, sine, cosine)
    sin_part = jnp.where(swap, cosine, sine)
    weight = jnp.where(frequency == 0, 1.0, 2.0) * (1.0 / math.sqrt(LAGS))
    cos_part = jnp.where(((quarter + 1) & 2) == 2, -cos_part, cos_part) * weight
    sin_part = jnp.where((quarter & 2) == 2, sin_part, -sin_part) * weight
    return cos_part.astype(jnp.bfloat16), sin_part.astype(jnp.bfloat16)


def pack_kernel(chans, band_ref, block_ref, flags_ref, x_ref, xs_ref, cand_ref, scale_ref, tier_ref, following, sems):
    depth = BINS * SLOTS
    f32, bf16 = jnp.float32, jnp.bfloat16

    following[SEG] = SEG

    def link(i, valid):
        g = SEG - 1 - i
        following[g] = jnp.where(flags_ref[g] > 0, g, following[g + 1])
        return valid + flags_ref[g]

    valid = lax.fori_loop(0, SEG, link, 0)

    def fetch(k, g):
        place = pl.ds(pl.multiple_of(k * BINS, BINS), BINS)
        return [
            pltpu.make_async_copy(x_ref.at[comp, g], xs_ref.at[comp, place, :], sems.at[comp, k]) for comp in range(2)
        ]

    def pack(k, at):
        for copy in fetch(k, jnp.minimum(at, SEG - 1)):
            copy.start()
        return following[jnp.minimum(at + 1, SEG)]

    def packed_slot(k, carry):
        for copy in fetch(k, 0):
            copy.wait()
        return carry

    tier = jnp.maximum((valid + 7) // 8 - 2, 0)
    tier_ref[0] = tier
    lax.fori_loop(0, 8 * (tier + 2), pack, following[0])
    lax.fori_loop(0, 8 * (tier + 2), packed_slot, 0)

    first = block_ref[0] * SRC
    width = RX * chans
    owner = first // width
    within = first - owner * width
    lane0 = pl.multiple_of(within // 128 * 128, 128)
    upper = (within // SRC) % 2
    sr = xs_ref[0, :, pl.ds(lane0, 128)].astype(f32)
    si = xs_ref[1, :, pl.ds(lane0, 128)].astype(f32)
    lane = lax.broadcasted_iota(jnp.int32, (depth, 128), 1)
    slot = lax.broadcasted_iota(jnp.int32, (depth, 128), 0) >> 4
    low = jnp.where(lane < SRC, sr, pltpu.roll(si, SRC, 1))
    high = jnp.where(lane < SRC, pltpu.roll(sr, SRC, 1), si)
    mine = jnp.where(upper == 0, low, high)
    count = jnp.where(owner == band_ref[0], valid, 0)
    mine = jnp.where(slot < count, mine, 0.0).astype(bf16)
    cand_ref[...] = mine
    scale_ref[...] = 1.0 / jnp.full((8, 128), valid, jnp.int32).astype(f32)


def stack_kernel(
    tiles, chans, bands,
    xs, cand, scale_ref, turned, table,
    send, recv, parts, own, zall, spread, cross,
    a2a_send, a2a_recv, rs_send, rs_recv, ag_send, ag_recv,
    right_send, right_recv, left_send, left_recv, sib_send, sib_recv,
):
    depth = BINS * 8 * tiles
    rows = depth // bands
    bins = BINS * chans
    half = chans // 2
    pieces = max(1, half // 8)
    size = half // pieces
    last = bands // 2
    groups = chans // 4
    c = lax.axis_index("chan")
    b = lax.axis_index("band")
    f32, bf16 = jnp.float32, jnp.bfloat16

    barrier = pltpu.get_barrier_semaphore()

    def greet_chan(i, carry):
        pl.semaphore_signal(barrier, inc=1, device_id=(lax.rem(c + i, chans), b), device_id_type=MESH)
        return carry

    def greet_band(i, carry):
        pl.semaphore_signal(barrier, inc=1, device_id=(c, lax.rem(b + i, bands)), device_id_type=MESH)
        return carry

    lax.fori_loop(1, bands, greet_band, 0)
    lax.fori_loop(1, chans, greet_chan, 0)

    def turn(block, carry):
        lanes = pl.ds(pl.multiple_of(block * 128, 128), 128)
        for comp in range(2):
            lines = xs[comp, :depth, lanes].T
            for q in range(4):
                send[4 * block + q, comp * RX:(comp + 1) * RX, :] = lines[q * RX:(q + 1) * RX]
        return carry

    lax.fori_loop(0, groups, turn, 0)
    recv[c] = send[c]

    pl.semaphore_wait(barrier, chans + bands - 2)

    def rs_copy(other, slot):
        return pltpu.make_async_remote_copy(
            src_ref=cand.at[pl.ds(pl.multiple_of(other * rows, rows), rows)], dst_ref=parts.at[slot],
            send_sem=rs_send.at[other], recv_sem=rs_recv.at[slot],
            device_id=(c, other), device_id_type=MESH)

    def rs_start(i, carry):
        rs_copy(lax.rem(b + i, bands), b).start()
        return carry

    lax.fori_loop(1, bands, rs_start, 0)

    def a2a_copy(dest, origin):
        return pltpu.make_async_remote_copy(
            src_ref=send.at[dest], dst_ref=recv.at[origin],
            send_sem=a2a_send.at[dest], recv_sem=a2a_recv.at[origin],
            device_id=(dest, b), device_id_type=MESH)

    def a2a_start(i, carry):
        a2a_copy(lax.rem(c + i, chans), c).start()
        return carry

    early = min(9, chans)
    lax.fori_loop(1, early, a2a_start, 0)

    count = min(32, bins // 2)

    def fill(i, carry):
        start = pl.multiple_of(i * count, count)
        for parity in range(2):
            cos_part, sin_part = lag_rows(parity, start, count)
            table[parity, pl.ds(start, count), :] = cos_part
            table[parity, pl.ds(bins // 2 + start, count), :] = sin_part
        return carry

    lax.fori_loop(0, bins // 2 // count, fill, 0)

    def rs_sum(i, total):
        other = lax.rem(b + i, bands)
        rs_copy(other, other).wait_recv()
        return total + parts[other].astype(f32)

    core = lax.rem(c, 2)
    twin = c + 1 - 2 * core
    holder = c // half
    own[...] = lax.fori_loop(1, bands, rs_sum, cand[pl.ds(pl.multiple_of(b * rows, rows), rows), :].astype(f32)).astype(bf16)

    @pl.when(holder == core)
    def _():
        zall[b, c] = own[...]

    def ag_copy(dest, origin):
        return pltpu.make_async_remote_copy(
            src_ref=own, dst_ref=zall.at[b, origin],
            send_sem=ag_send.at[dest // 2], recv_sem=ag_recv.at[origin],
            device_id=(dest, b), device_id_type=MESH)

    def ag_dest(i):
        return 2 * lax.rem(c // 2 + i, half) + holder

    def ag_start(i, carry):
        dest = ag_dest(i)

        @pl.when(dest != c)
        def _():
            ag_copy(dest, c).start()
        return carry

    lax.fori_loop(0, half, ag_start, 0)

    def ag_wait(start, number):
        def one(i, carry):
            @pl.when(start + i != c)
            def _():
                ag_copy(start + i, start + i).wait_recv()
            return carry

        lax.fori_loop(0, number, one, 0)

    right = lax.rem(b + 1, bands)
    left = lax.rem(b + bands - 1, bands)

    def part(origin, owner, piece, step, way):
        start, number = half * owner + size * piece, size
        if step == last:
            number = size // 2
            if way < 0:
                start = start + number
        return zall.at[origin, pl.ds(start, number)]

    def hop(piece, step, way, which):
        origin = lax.rem(b + bands - way * (step - 1 + which), bands)
        ref = part(origin, core, piece, step, way)
        sems = (right_send, right_recv) if way > 0 else (left_send, left_recv)
        return pltpu.make_async_remote_copy(
            src_ref=ref, dst_ref=ref, send_sem=sems[0].at[piece, step - 1], recv_sem=sems[1].at[piece, step - 1],
            device_id=(c, right if way > 0 else left), device_id_type=MESH)

    def share(piece, step, way, mine):
        origin = lax.rem(b + bands - way * step, bands)
        ref = part(origin, core if mine else 1 - core, piece, step, way)
        k = 2 * step - (1 if way > 0 else 0) if step else 0
        return pltpu.make_async_remote_copy(
            src_ref=ref, dst_ref=ref, send_sem=sib_send.at[piece, k], recv_sem=sib_recv.at[piece, k],
            device_id=(twin, b), device_id_type=MESH)

    def begin(piece):
        ag_wait(half * core + size * piece, size)
        for way in (1, -1):
            hop(piece, 1, way, 0).start()
        share(piece, 0, 1, True).start()

    def advance(piece, step):
        for way in (1, -1):
            hop(piece, step - 1, way, 1).wait_recv()
            if step <= last:
                hop(piece, step, way, 0).start()
            share(piece, step - 1, way, True).start()

    def arrived(piece):
        share(piece, 0, 1, False).wait_recv()
        for step in range(1, last + 1):
            for way in (1, -1):
                share(piece, step, way, False).wait_recv()

    inverse = jnp.broadcast_to(scale_ref[0:1, :], (8 * BINS, 128))
    row = lax.broadcasted_iota(jnp.int32, (BINS, depth), 0)
    row_bin = jnp.where(row < BINS // 2, 2 * row, 2 * row - (BINS - 1))
    kept = row_bin == (lax.broadcasted_iota(jnp.int32, (BINS, depth), 1) & (BINS - 1))
    sign = jnp.where(lax.broadcasted_iota(jnp.int32, (1, 128), 1) < SRC, 1.0, -1.0)

    def stack(j, buffer):
        z = zall[:, j].reshape(depth, 128)
        swapped = (pltpu.roll(z.astype(f32), SRC, 1) * sign).astype(bf16)
        weights = jnp.concatenate([z, swapped], axis=0)
        spread[buffer] = recv[j].astype(f32)
        place = pl.ds(pl.multiple_of(BINS // 2 * j, BINS // 2), BINS // 2)
        for g in range(RX // 8):
            left = []
            for r in range(8 * g, 8 * g + 8):
                line = []
                for comp in range(2):
                    value = jnp.broadcast_to(spread[buffer, comp * RX + r:comp * RX + r + 1, :], (BINS, depth))
                    line.append(jnp.where(kept, value, 0.0).astype(bf16))
                left.append(jnp.concatenate(line, axis=1))
            product = jnp.dot(jnp.concatenate(left, axis=0), weights, preferred_element_type=f32) * inverse
            product = product.reshape(8, BINS, 128)
            cross[0, 8 * g:8 * g + 8, place, :] = product[:, :BINS // 2]
            cross[1, 8 * g:8 * g + 8, place, :] = product[:, BINS // 2:]

    def stack_piece(owner, piece):
        few = min(size, 4)

        def group(g, carry):
            start = half * owner + size * piece + few * g

            def a2a_wait(i, inner):
                @pl.when(start + i != c)
                def _():
                    a2a_copy(start + i, start + i).wait_recv()
                return inner

            lax.fori_loop(0, few, a2a_wait, 0)
            for k in range(few):
                stack(start + k, k)
            return carry

        lax.fori_loop(0, size // few, group, 0)

    def finish(piece):
        arrived(piece)

        def both(owner, carry):
            stack_piece(owner, piece)
            return carry

        lax.fori_loop(0, 2, both, 0)

    for piece in range(pieces):
        begin(piece)
    lax.fori_loop(early, chans, a2a_start, 0)
    for step in range(2, last + 2):
        for piece in range(pieces):
            advance(piece, step)
    for piece in range(pieces):
        finish(piece)

    k = bins // 2
    for g in range(RX // 8):
        def turn_back(i, carry, g=g):
            for r in (2 * i, 2 * i + 1):
                for parity in range(2):
                    flat = cross[parity, 8 * g + r].astype(bf16).T
                    turned[8 * g + r, :, 2 * parity * k:(2 * parity + 1) * k] = flat[:SRC]
                    turned[8 * g + r, :, (2 * parity + 1) * k:(2 * parity + 2) * k] = flat[SRC:]
            return carry

        lax.fori_loop(0, 4, turn_back, 0)

    def rs_done(i, carry):
        rs_copy(lax.rem(b + i, bands), b).wait_send()
        return carry

    def chan_done(i, carry):
        other = lax.rem(c + i, chans)
        a2a_copy(other, c).wait_send()
        return carry

    def ag_done(i, carry):
        dest = ag_dest(i)

        @pl.when(dest != c)
        def _():
            ag_copy(dest, c).wait_send()
        return carry

    lax.fori_loop(1, bands, rs_done, 0)
    lax.fori_loop(1, chans, chan_done, 0)
    lax.fori_loop(0, half, ag_done, 0)
    for piece in range(pieces):
        share(piece, 0, 1, True).wait_send()
        for step in range(1, last + 1):
            for way in (1, -1):
                hop(piece, step, way, 0).wait_send()
                share(piece, step, way, True).wait_send()


def packed(chans, block, flags, x):
    vmem = pl.BlockSpec(memory_space=pltpu.VMEM)
    smem = pl.BlockSpec(memory_space=pltpu.SMEM)
    depth = BINS * SLOTS
    return pl.pallas_call(
        functools.partial(pack_kernel, chans),
        out_shape=(
            jax.ShapeDtypeStruct((2, depth, RX * chans), jnp.bfloat16),
            jax.ShapeDtypeStruct((depth, 128), jnp.bfloat16),
            jax.ShapeDtypeStruct((8, 128), jnp.float32),
            jax.ShapeDtypeStruct((1,), jnp.int32),
        ),
        in_specs=[smem, smem, smem, pl.BlockSpec(memory_space=pltpu.HBM)],
        out_specs=(vmem, vmem, vmem, smem),
        scratch_shapes=[pltpu.SMEM((SLOTS,), jnp.int32), pltpu.SemaphoreType.DMA((2, SLOTS))],
        compiler_params=pltpu.CompilerParams(vmem_limit_bytes=60 * 1024 * 1024),
    )(lax.axis_index("band").reshape(1), block, flags, x)


def stacked(tiles, chans, bands, xs, cand, scale):
    depth = BINS * 8 * tiles
    rows = depth // bands
    bins = BINS * chans
    pieces = max(1, chans // 16)
    last = bands // 2
    dma = pltpu.SemaphoreType.DMA
    f32, bf16 = jnp.float32, jnp.bfloat16
    vmem = pl.BlockSpec(memory_space=pltpu.VMEM)
    flops = 2 * chans * RX * BINS * 2 * depth * 128
    return pl.pallas_call(
        functools.partial(stack_kernel, tiles, chans, bands),
        out_shape=(
            jax.ShapeDtypeStruct((RX, SRC, 2 * bins), bf16),
            jax.ShapeDtypeStruct((2, bins, LAGS // 2), bf16),
        ),
        in_specs=[vmem] * 3,
        out_specs=(vmem, vmem),
        scratch_shapes=[
            pltpu.VMEM((chans, 2 * RX, depth), bf16),
            pltpu.VMEM((chans, 2 * RX, depth), bf16),
            pltpu.VMEM((bands, rows, 128), bf16),
            pltpu.VMEM((rows, 128), bf16),
            pltpu.VMEM((bands, chans, rows, 128), bf16),
            pltpu.VMEM((4, 2 * RX, depth), f32),
            pltpu.VMEM((2, RX, bins // 2, 128), f32),
            dma((chans,)), dma((chans,)), dma((bands,)), dma((bands,)), dma((chans // 2,)), dma((chans,)),
            dma((pieces, last)), dma((pieces, last)), dma((pieces, last)), dma((pieces, last)),
            dma((pieces, 2 * last + 1)), dma((pieces, 2 * last + 1)),
        ],
        compiler_params=pltpu.CompilerParams(
            collective_id=tiles, has_side_effects=True, vmem_limit_bytes=36 * 1024 * 1024
        ),
        cost_estimate=pl.CostEstimate(flops=flops, bytes_accessed=8 * 1024 * 1024, transcendentals=0),
    )(xs, cand, scale)


def lag_kernel(cross_ref, weights_ref, out_ref):
    k = weights_ref.shape[1]
    for q in range(SRC // BINS):
        sources = slice(BINS * q, BINS * q + BINS)
        left = cross_ref[:, sources, :].reshape(RX * BINS, 2 * k)
        even = jnp.dot(left[:, :k], weights_ref[0], preferred_element_type=jnp.float32)
        odd = jnp.dot(left[:, k:], weights_ref[1], preferred_element_type=jnp.float32)
        low = (even + odd).reshape(RX, BINS, LAGS // 2)
        high = (even - odd).reshape(RX, BINS, LAGS // 2)
        for r in range(RX):
            out_ref[sources, 0, r, :LAGS // 2] = low[r]
            out_ref[sources, 0, r, LAGS // 2:] = high[r]


def correlate(cross, weights):
    k = weights.shape[1]
    vmem = pl.BlockSpec(memory_space=pltpu.VMEM)
    return pl.pallas_call(
        lag_kernel,
        out_shape=jax.ShapeDtypeStruct((SRC, 1, RX, LAGS), jnp.float32),
        in_specs=[vmem] * 2,
        out_specs=vmem,
        compiler_params=pltpu.CompilerParams(vmem_limit_bytes=32 * 1024 * 1024),
        cost_estimate=pl.CostEstimate(
            flops=2 * SRC * RX * k * LAGS, bytes_accessed=16 * 1024 * 1024, transcendentals=0
        ),
    )(cross, weights)


def solution(mesh):
    chans, bands = mesh.shape["chan"], mesh.shape["band"]

    def local(spectra, source_block, segment_flags):
        *operands, tier = packed(chans, source_block, segment_flags, spectra)

        def branch(tiles):
            return lambda *arrays: correlate(*stacked(tiles, chans, bands, *arrays))

        return lax.switch(tier[0], [branch(tiles) for tiles in (2, 3, 4)], *operands)

    return jax.shard_map(
        local,
        mesh=mesh,
        in_specs=(P(None, None, "chan", "band"), P(), P()),
        out_specs=P(None, "band", "chan", None),
        check_vma=False,
    )
```
